128 devices in a mesh: space: 16 (over y_hi, z, core), member: 8 (over x, y_lo).
Axes of the slice: x: 4, y: 4 (y_hi: 2, y_lo: 2; y = y_hi * 2 + y_lo), z: 4, core: 2. Of those that a mesh axis runs over, the one named last changes fastest.
Arguments:
- tokens: bfloat16 [16, 32, 256, 1536], P('member', 'space'), may hold values from -6 to 6
- gain: float32 [1536], replicated, may hold values from 0.5 to 1.5
- weight: bfloat16 [1536, 1120], P(('space', 'member')), may hold values from -0.15625 to 0.15625
- bias: float32 [1120], replicated, may hold values from -3 to 3
- target: bfloat16 [70, 128, 1024], P(None, 'space'), may hold values from -6 to 6
- channel_weight: float32 [70], replicated, may hold values from 0.5 to 2
Outputs:
- token_gradient: bfloat16 [16, 32, 256, 1536], P('member', 'space')
- gain_gradient: float32 [1536], replicated
- grad_weight: float32 [1536, 1120], P(('space', 'member'))
- grad_bias: float32 [1120], replicated
The draws below stay inside these ranges and needn't reach their ends.
All inputs are finite; a program needn't handle non-finite values.
Results may differ from the reference program's by a relative error of at most 0.023.
Values may be sent and summed in bfloat16 or wider, within the bound.
No kernel may reach another device: no remote copies, remote signals or barrier semaphores. Data moves between devices by JAX's collectives and lax.ppermute only.
A program may use at most 192 MiB of HBM per device.

```python
import math
import jax
import jax.numpy as jnp
from jax import lax

D = 1536
CH = 70
LON_TOK = 256
OUT = 1120
MEMBERS = 16
TOK_LAT = 32
GRID_LAT = 128
GRID_LON = 1024


def shard_levels(rng, dims, split, low, high):
    def one(position, shards_of):
        draws = jax.random.uniform(jax.random.fold_in(jax.random.fold_in(rng, 6), position), (shards_of,), jnp.float32, low / len(split), high / len(split))
        return jnp.repeat(jnp.exp(draws), dims[position] // shards_of).reshape((-1,) + (1,) * (len(dims) - position - 1))

    level = one(*split[0])
    for cut in split[1:]:
        level = level * one(*cut)
    return level


def bell_draw(key, extent, deviation, reach, shards=(), kind=jnp.bfloat16):
    loudness = shard_levels(key, extent, shards, -0.22, 0.18) if shards else 1.0
    drawn = jax.random.normal(key, extent, jnp.float32) * deviation * loudness
    return jnp.minimum(jnp.maximum(drawn, -reach), reach).astype(kind)


def setup_inputs(seed: int = 0) -> dict:
    key_list = jax.random.split(jax.random.key(seed), 7)
    tokens = bell_draw(key_list[0], (MEMBERS, TOK_LAT, LON_TOK, D), 1.0, 6.0, ((0, 8), (1, 16)))
    gain = jnp.clip(1.0 + 0.1 * jax.random.normal(key_list[1], (D,), jnp.float32), 0.5, 1.5)
    weight = bell_draw(key_list[2], (D, OUT), D ** -0.5, 0.15625, ((0, 128),))
    bias = bell_draw(key_list[3], (OUT,), 0.5, 3.0, (), jnp.float32)
    target = bell_draw(key_list[4], (CH, GRID_LAT, GRID_LON), 1.0, 6.0, ((1, 16),))
    channel_weight = jnp.clip(jnp.exp(jax.random.uniform(key_list[5], (CH,), jnp.float32, math.log(0.5), math.log(2.0))), 0.5, 2.0)
    return dict(tokens=tokens, gain=gain, weight=weight, bias=bias, target=target, channel_weight=channel_weight)


ALPHA = 0.95
DELTA = 0.1
EPS = 1e-05

def latitude_weights(rows):
    index = jnp.arange(rows, dtype=jnp.float32)
    angle = (60.0 - 0.25 * (index + 0.5)) * (jnp.pi / 180.0)
    cosine = jnp.cos(angle)
    return cosine / jnp.mean(cosine)

def token_layout(target):
    chans, grid_rows, grid_cols = target.shape
    shaped = target.reshape(chans, grid_rows // 4, 4, grid_cols // 4, 4)
    shaped = jnp.transpose(shaped, (1, 3, 0, 2, 4))
    return shaped.reshape(grid_rows // 4, grid_cols // 4, chans * 16)

def slope(value):
    return value * lax.rsqrt(value * value + DELTA * DELTA)

def reference(tokens, gain, weight, bias, target, channel_weight):
    count = MEMBERS
    eps_fair = (1.0 - ALPHA) / count
    coef = (1.0 - eps_fair) / (count * (count - 1))
    chans = channel_weight.shape[0]
    lat_rows = tokens.shape[1]
    wide = tokens.astype(jnp.float32)
    feature_mean = lax.optimization_barrier(jnp.mean(wide, -1, keepdims=True))
    centred_input = wide - feature_mean
    variance = lax.optimization_barrier(jnp.mean(centred_input * centred_input, -1, keepdims=True))
    inverse_deviation = lax.rsqrt(variance + EPS)
    standardized_input = centred_input * inverse_deviation
    normed_tokens = (standardized_input * gain).astype(jnp.bfloat16)
    weight_wide = weight.astype(jnp.float32)

    def project(rows):
        return (jnp.einsum('tld,do->tlo', rows.astype(jnp.float32), weight_wide) + bias).astype(jnp.bfloat16)
    field = lax.map(project, normed_tokens)
    truth = token_layout(target).astype(jnp.float32)
    latw = latitude_weights(4 * lat_rows).reshape(lat_rows, 4)
    table = jnp.broadcast_to(channel_weight[None, :, None, None] * latw[:, None, :, None], (lat_rows, chans, 4, 4))
    weights = table.reshape(lat_rows, 1, chans * 16)
    fields = field.astype(jnp.float32)

    def member_grad(mine):

        def add(total, other):
            return (total + slope(mine - other), None)
        pairs, _ = lax.scan(add, jnp.zeros_like(mine), fields)
        return (weights * (slope(mine - truth) / count - coef * pairs)).astype(jnp.bfloat16)
    dfield = lax.map(member_grad, fields)
    dwide = dfield.astype(jnp.float32)
    grad_bias = lax.optimization_barrier(jnp.sum(dwide, axis=(0, 1, 2)))
    grad_weight = jnp.einsum('mtld,mtlo->do', normed_tokens.astype(jnp.float32), dwide)
    normed_gradient = jnp.einsum('mtlo,do->mtld', dwide, weight_wide)
    gain_gradient = lax.optimization_barrier(jnp.sum(normed_gradient * standardized_input, axis=(0, 1, 2)))
    scaled_tokens = normed_gradient * gain
    token_gradient = inverse_deviation * (scaled_tokens - lax.optimization_barrier(jnp.mean(scaled_tokens, -1, keepdims=True)) - standardized_input * lax.optimization_barrier(jnp.mean(scaled_tokens * standardized_input, -1, keepdims=True)))
    return (token_gradient.astype(jnp.bfloat16), gain_gradient, grad_weight, grad_bias)
```

```python
import functools

import jax
import jax.numpy as jnp
import numpy as np
from jax import lax
from jax.experimental import pallas as pl
from jax.experimental.pallas import tpu as pltpu
from jax.sharding import Mesh
from jax.sharding import PartitionSpec as P

ALPHA = 0.95
DELTA = 0.1
EPS = 1e-05
SIZE = dict(yh=2, z=4, core=2, x=4, yl=2)
SPACE = ("yh", "z", "core")
MEMBER = ("x", "yl")
CHUNKS = ((0, 640), (640, 480))
BF16 = jnp.bfloat16
F32 = jnp.float32
PARAMS = pltpu.CompilerParams(vmem_limit_bytes=56 * 1024 * 1024)


def latitude_weights(rows):
    index = np.arange(rows, dtype=np.float64)
    cosine = np.cos((60.0 - 0.25 * (index + 0.5)) * (np.pi / 180.0))
    return (cosine / cosine.mean()).astype(np.float32)


def swap(value, axis, step):
    return lax.ppermute(value, axis, [(i, i ^ step) for i in range(SIZE[axis])])


def swap_member(value, step):
    return lax.ppermute(value, MEMBER, [(i, i ^ step) for i in range(8)])


def vmem(count):
    return [pl.BlockSpec(memory_space=pltpu.VMEM)] * count


def truth_kernel(image_ref, out_ref):
    image = image_ref[...]
    chan_rows, cols = image.shape
    cells = cols // 4
    outs = chan_rows * 4
    total = jnp.zeros((cells, outs), F32)
    for q in range(4):
        pick = (
            lax.broadcasted_iota(jnp.int32, (cells, cols), 1)
            == 4 * lax.broadcasted_iota(jnp.int32, (cells, cols), 0) + q
        ).astype(BF16)
        part = lax.dot_general(
            pick, image, (((1,), (1,)), ((), ())), preferred_element_type=F32
        ).astype(BF16)
        place = (
            lax.broadcasted_iota(jnp.int32, (chan_rows, outs), 1)
            == 4 * lax.broadcasted_iota(jnp.int32, (chan_rows, outs), 0) + q
        ).astype(BF16)
        total = total + jnp.dot(part, place, preferred_element_type=F32)
    out_ref[...] = total


def norm_kernel(tokens_ref, gain_ref, normed_ref):
    wide = tokens_ref[...].astype(F32)
    mean = jnp.mean(wide, -1, keepdims=True)
    centred = wide - mean
    variance = jnp.mean(centred * centred, -1, keepdims=True)
    normed_ref[...] = (centred * lax.rsqrt(variance + EPS) * gain_ref[...]).astype(BF16)


def weight_kernel(place_ref, a_ref, b_ref, c_ref, d_ref, out_ref):
    for core, yh, ref in ((0, 0, a_ref), (0, 1, b_ref), (1, 0, c_ref), (1, 1, d_ref)):
        for step in range(4):
            block = (
                (place_ref[0] ^ yh) * 8 + (place_ref[1] ^ step) * 2 + (place_ref[2] ^ core)
            )
            out_ref[pl.ds(pl.multiple_of(block * 96, 96), 96), :] = ref[step]


def slope(value):
    return value * lax.rsqrt(value * value + DELTA * DELTA)


def middle_kernel(
    place_ref, normed_ref, weight_ref, bias_ref, truth_ref, wt_ref,
    dfield_ref, bias_out_ref, keep_ref, send_ref, field, grad, sums,
):
    width = weight_ref.shape[1]
    padded = field.shape[2]
    count = 16
    coef = (1.0 - (1.0 - ALPHA) / count) / (count * (count - 1))

    def project(step, carry):
        row = pl.multiple_of(step * 256, 256)
        part = jnp.dot(
            normed_ref[pl.ds(row, 256), :], weight_ref[...], preferred_element_type=F32
        ) + bias_ref[...]
        part = part.astype(BF16).astype(F32).reshape(4, 64, width)
        field[pl.ds(step * 4, 4), :, 0:width] = part
        return carry

    lax.fori_loop(0, 4, project, 0)
    sums[...] = jnp.zeros_like(sums)

    def pairs(step, carry):
        row = pl.multiple_of((step // (padded // 128)) * 8, 8)
        lane = pl.multiple_of((step % (padded // 128)) * 128, 128)
        here = (pl.ds(row, 8), pl.ds(lane, 128))
        values = [field[m, here[0], here[1]] for m in range(count)]
        total = [None] * count
        for m in range(count):
            for k in range(m + 1, count):
                s = slope(values[m] - values[k])
                total[m] = s if total[m] is None else total[m] + s
                total[k] = -s if total[k] is None else total[k] - s
        true = truth_ref[here[0], here[1]]
        scale = wt_ref[0:1, pl.ds(lane, 128)]
        column = None
        for m in range(count):
            value = scale * (slope(values[m] - true) * (1.0 / count) - coef * total[m])
            value = value.astype(BF16).astype(F32)
            field[m, here[0], here[1]] = value
            column = value if column is None else column + value
        sums[:, pl.ds(lane, 128)] += column
        return carry

    lax.fori_loop(0, 8 * (padded // 128), pairs, 0)
    bias_out_ref[...] = sums[:, 0:width]

    def store(step, carry):
        row = pl.multiple_of(step * 64, 64)
        dfield_ref[pl.ds(row, 64), :] = field[step, :, 0:width].astype(BF16)
        return carry

    lax.fori_loop(0, count, store, 0)

    def weight_grad(step, carry):
        lane = pl.multiple_of(step * 256, 256)
        grad[pl.ds(lane, 256), :] = lax.dot_general(
            normed_ref[:, pl.ds(lane, 256)],
            dfield_ref[...],
            (((0,), (0,)), ((), ())),
            preferred_element_type=F32,
        )
        return carry

    lax.fori_loop(0, 6, weight_grad, 0)
    for yh in range(2):
        for step in range(4):
            base = (place_ref[0] ^ yh) * 8 + (place_ref[1] ^ step) * 2
            mine = pl.multiple_of((base + place_ref[2]) * 96, 96)
            other = pl.multiple_of((base + (place_ref[2] ^ 1)) * 96, 96)
            keep_ref[yh, step] = grad[pl.ds(mine, 96), :]
            send_ref[yh, step] = grad[pl.ds(other, 96), :].astype(BF16)


def backward_kernel(tokens_ref, gain_ref, *refs):
    count = len(CHUNKS)
    dfields, weights = refs[:count], refs[count : 2 * count]
    out_ref, gain_out_ref = refs[2 * count :]
    step = pl.program_id(0)
    wide = tokens_ref[...].astype(F32)
    mean = jnp.mean(wide, -1, keepdims=True)
    centred = wide - mean
    variance = jnp.mean(centred * centred, -1, keepdims=True)
    inverse = lax.rsqrt(variance + EPS)
    xhat = centred * inverse
    grad = None
    for d_ref, w_ref in zip(dfields, weights):
        part = lax.dot_general(
            d_ref[...], w_ref[...], (((1,), (1,)), ((), ())), preferred_element_type=F32
        )
        grad = part if grad is None else grad + part

    @pl.when(step == 0)
    def _():
        gain_out_ref[...] = jnp.zeros_like(gain_out_ref)

    rows = grad.shape[0]
    gain_out_ref[...] += jnp.sum((grad * xhat).reshape(rows // 8, 8, -1), axis=0)
    scaled = grad * gain_ref[...]
    out = inverse * (
        scaled
        - jnp.mean(scaled, -1, keepdims=True)
        - xhat * jnp.mean(scaled * xhat, -1, keepdims=True)
    )
    out_ref[...] = out.astype(BF16)


def gather_weight(weight, where):
    pieces = [weight] + [swap(weight, "x", k) for k in (1, 2, 3)]
    near = jnp.stack(pieces)
    both = jnp.stack([near, swap(near, "yl", 1)], axis=1)
    rows, width = weight.shape
    members = 8 * rows
    index = jnp.arange(members)
    block, inside = index // rows, index % rows
    source = (((block // 2) ^ where["x"]) * 2 + ((block % 2) ^ where["yl"])) * rows + inside
    pick = (source[:, None] == jnp.arange(members)[None, :]).astype(BF16)
    block = jnp.dot(
        pick, both.reshape(members, width), preferred_element_type=F32
    ).astype(BF16)
    pair = [block, swap(block, "yh", 1)]
    pair = jnp.stack(pair)
    quad = [pair] + [swap(pair, "z", k) for k in (1, 2, 3)]
    quad = jnp.stack(quad, axis=1)
    other = swap(quad, "core", 1)
    place = jnp.stack([where["yh"], where["z"], where["core"]]).astype(jnp.int32)
    full = pl.pallas_call(
        weight_kernel,
        out_shape=jax.ShapeDtypeStruct((16 * members, width), BF16),
        in_specs=[pl.BlockSpec(memory_space=pltpu.SMEM)] + vmem(4),
        out_specs=pl.BlockSpec(memory_space=pltpu.VMEM),
        compiler_params=PARAMS,
        name="weight_rows",
    )(place, quad[0], quad[1], other[0], other[1])
    return full, place


def scatter_grad(keep, send, where):
    width = keep.shape[-1]
    total = keep + swap(send, "core", 1).astype(F32)
    low = total.astype(BF16)
    total = sum([swap(low[:, k], "z", k).astype(F32) for k in (1, 2, 3)], total[:, 0])
    total = total[0] + swap(total[1].astype(BF16), "yh", 1).astype(F32)
    total = total.reshape(4, 2, 12, width)

    def part(value, index):
        return lax.dynamic_index_in_dim(value, index, 0, keepdims=False)

    mine = part(total, where["x"])
    for k in (1, 2, 3):
        mine = mine + swap(part(total, where["x"] ^ k).astype(BF16), "x", k).astype(F32)
    return part(mine, where["yl"]) + swap(
        part(mine, where["yl"] ^ 1).astype(BF16), "yl", 1
    ).astype(F32)


def all_sum(value):
    for axis in ("core", "z", "yh", "x", "yl"):
        value = sum([swap(value, axis, k) for k in range(1, SIZE[axis])], value)
    return value


def on_device(tokens, gain, weight, bias, target, channel_weight):
    where = {axis: lax.axis_index(axis) for axis in SIZE}
    member = where["x"] * 2 + where["yl"]
    space = (where["yh"] * 4 + where["z"]) * 2 + where["core"]
    features = tokens.shape[-1]
    outs = weight.shape[1]

    full, place = gather_weight(weight, where)
    pieces = tokens.reshape(2, 8, 64, features)
    received = []
    for k in range(8):
        piece = lax.dynamic_index_in_dim(pieces, member ^ k, 1, keepdims=False)
        received.append(swap_member(piece, k) if k else piece)
    gathered = jnp.concatenate([r.reshape(128, features) for r in received])

    t_here, l_here = member // 4, member % 4
    image = lax.dynamic_slice(
        target, (0, 4 * t_here, 256 * l_here), (target.shape[0], 4, 256)
    ).reshape(-1, 256)
    truth = pl.pallas_call(
        truth_kernel,
        out_shape=jax.ShapeDtypeStruct((64, outs), F32),
        in_specs=vmem(1),
        out_specs=vmem(1)[0],
        compiler_params=PARAMS,
        name="truth",
    )(image)
    table = jnp.asarray(latitude_weights(128).reshape(32, 4))
    latw = lax.dynamic_index_in_dim(table, space * 2 + t_here, 0, keepdims=False)
    wt = jnp.broadcast_to(
        channel_weight[:, None, None] * latw[None, :, None], (channel_weight.shape[0], 4, 4)
    ).reshape(1, outs)

    gain_row = gain.reshape(1, features)
    bias_row = bias.reshape(1, outs)
    normed = pl.pallas_call(
        norm_kernel,
        grid=(4,),
        out_shape=jax.ShapeDtypeStruct((1024, features), BF16),
        in_specs=[
            pl.BlockSpec((256, features), lambda i: (i, 0)),
            pl.BlockSpec((1, features), lambda i: (0, 0)),
        ],
        out_specs=pl.BlockSpec((256, features), lambda i: (i, 0)),
        compiler_params=PARAMS,
        name="norm",
    )(gathered, gain_row)

    dfields, weights, bias_parts, shares = [], [], [], []
    for start, width in CHUNKS:
        padded = -(-width // 128) * 128
        cut = slice(start, start + width)
        chunk = full[:, cut]
        pad = ((0, 0), (0, padded - width))
        dfield, bias_part, keep, send = pl.pallas_call(
            middle_kernel,
            out_shape=(
                jax.ShapeDtypeStruct((1024, width), BF16),
                jax.ShapeDtypeStruct((8, width), F32),
                jax.ShapeDtypeStruct((2, 4, 96, width), F32),
                jax.ShapeDtypeStruct((2, 4, 96, width), BF16),
            ),
            in_specs=[pl.BlockSpec(memory_space=pltpu.SMEM)] + vmem(5),
            out_specs=tuple(vmem(4)),
            scratch_shapes=[
                pltpu.VMEM((16, 64, padded), F32),
                pltpu.VMEM((features, width), F32),
                pltpu.VMEM((8, padded), F32),
            ],
            compiler_params=PARAMS,
            name="middle",
        )(
            place, normed, chunk, bias_row[:, cut],
            jnp.pad(truth[:, cut], pad), jnp.pad(wt[:, cut], pad),
        )
        dfields.append(dfield)
        weights.append(chunk)
        bias_parts.append(bias_part)
        shares.append(scatter_grad(keep, send, where))

    token_part, gain_part = pl.pallas_call(
        backward_kernel,
        grid=(8,),
        out_shape=(
            jax.ShapeDtypeStruct((1024, features), BF16),
            jax.ShapeDtypeStruct((8, features), F32),
        ),
        in_specs=[
            pl.BlockSpec((128, features), lambda i: (i, 0)),
            pl.BlockSpec((1, features), lambda i: (0, 0)),
        ]
        + [pl.BlockSpec((128, w), lambda i: (i, 0)) for _, w in CHUNKS]
        + [pl.BlockSpec((features, w), lambda i: (0, 0)) for _, w in CHUNKS],
        out_specs=(
            pl.BlockSpec((128, features), lambda i: (i, 0)),
            pl.BlockSpec((8, features), lambda i: (0, 0)),
        ),
        compiler_params=PARAMS,
        name="backward",
    )(gathered, gain_row, *dfields, *weights)

    small = jnp.concatenate(
        [jnp.sum(gain_part, axis=0)] + [jnp.sum(part, axis=0) for part in bias_parts]
    )
    small = jnp.pad(small, (0, 3072 - small.shape[0])).reshape(24, 128)
    small = all_sum(small).reshape(-1)

    back = token_part.reshape(8, 2, 64, features)
    result = jnp.zeros((2, 8, 64, features), BF16)
    for k in range(8):
        piece = swap_member(back[k], k) if k else back[k]
        result = lax.dynamic_update_slice(result, piece[:, None], (0, member ^ k, 0, 0))
    return (
        result.reshape(tokens.shape),
        small[:features],
        jnp.concatenate(shares, axis=1),
        small[features : features + outs],
    )


def solution(mesh):
    fine = Mesh(
        mesh.devices.reshape(2, 4, 2, 4, 2), ("yh", "z", "core", "x", "yl")
    )
    both = SPACE + MEMBER
    return jax.shard_map(
        on_device,
        mesh=fine,
        in_specs=(
            P(MEMBER, SPACE, None, None),
            P(),
            P(both, None),
            P(),
            P(None, SPACE, None),
            P(),
        ),
        out_specs=(P(MEMBER, SPACE, None, None), P(), P(both, None), P()),
        check_vma=False,
    )
```

```python
import functools

import jax
import jax.numpy as jnp
import numpy as np
from jax import lax
from jax.experimental import pallas as pl
from jax.experimental.pallas import tpu as pltpu
from jax.sharding import Mesh
from jax.sharding import PartitionSpec as P

ALPHA = 0.95
DELTA = 0.1
EPS = 1e-05
SIZE = dict(yh=2, z=4, core=2, x=4, yl=2)
SPACE = ("yh", "z", "core")
MEMBER = ("x", "yl")
BF16 = jnp.bfloat16
F32 = jnp.float32


def params(mebibytes):
    return pltpu.CompilerParams(vmem_limit_bytes=mebibytes * 1024 * 1024)


def cost(flops, bytes_accessed):
    return pl.CostEstimate(flops=flops, bytes_accessed=bytes_accessed, transcendentals=0)


def after(values, *done):
    out = lax.optimization_barrier((*values, *done))
    return out[: len(values)], out[len(values) :]


def latitude_weights(rows):
    index = np.arange(rows, dtype=np.float64)
    cosine = np.cos((60.0 - 0.25 * (index + 0.5)) * (np.pi / 180.0))
    return (cosine / cosine.mean()).astype(np.float32)


def swap(value, axis, step):
    return lax.ppermute(value, axis, [(i, i ^ step) for i in range(SIZE[axis])])


def swap_y(value, step):
    return lax.ppermute(value, ("yh", "yl"), [(i, i ^ step) for i in range(4)])


def swap_member(value, step):
    return lax.ppermute(value, MEMBER, [(i, i ^ step) for i in range(8)])


def vmem(count):
    return [pl.BlockSpec(memory_space=pltpu.VMEM)] * count


def truth_kernel(image_ref, out_ref):
    image = image_ref[...]
    chan_rows, cols = image.shape
    cells = cols // 4
    total = jnp.zeros(out_ref.shape, F32)
    for q in range(4):
        pick = (
            lax.broadcasted_iota(jnp.int32, (cells, cols), 1)
            == 4 * lax.broadcasted_iota(jnp.int32, (cells, cols), 0) + q
        ).astype(BF16)
        part = lax.dot_general(
            pick, image, (((1,), (1,)), ((), ())), preferred_element_type=F32
        ).astype(BF16)
        place = (
            lax.broadcasted_iota(jnp.int32, (chan_rows, total.shape[1]), 1)
            == 4 * lax.broadcasted_iota(jnp.int32, (chan_rows, total.shape[1]), 0) + q
        ).astype(BF16)
        total = total + jnp.dot(part, place, preferred_element_type=F32)
    out_ref[...] = total


def norm_kernel(tokens_ref, gain_ref, normed_ref, flipped_ref):
    wide = tokens_ref[...].astype(F32)
    mean = jnp.mean(wide, -1, keepdims=True)
    centred = wide - mean
    variance = jnp.mean(centred * centred, -1, keepdims=True)
    normed = (centred * lax.rsqrt(variance + EPS) * gain_ref[...]).astype(BF16)
    normed_ref[...] = normed
    flipped_ref[...] = normed.T


def norm_piece(piece, gain_row):
    features = piece.shape[-1]
    return pl.pallas_call(
        norm_kernel,
        out_shape=(
            jax.ShapeDtypeStruct((128, features), BF16),
            jax.ShapeDtypeStruct((features, 128), BF16),
        ),
        in_specs=vmem(2),
        out_specs=tuple(vmem(2)),
        compiler_params=params(8),
        cost_estimate=cost(2000000000, 8000000),
        name="norm",
    )(piece.reshape(128, features), gain_row)


def slope(value):
    return value * lax.rsqrt(value * value + DELTA * DELTA)


def pairs_kernel(
    place_ref, quad_ref, other_ref, bias_ref, truth_ref, wt_ref, *refs
):
    pieces = refs[:8]
    full_ref, dfield_ref, bias_out_ref, normed_ref, field, sums = refs[8:]
    for k in range(8):
        normed_ref[pl.ds(128 * k, 128), :] = pieces[k][...]
    width = full_ref.shape[1]
    padded = field.shape[2]
    count = 16
    coef = (1.0 - (1.0 - ALPHA) / count) / (count * (count - 1))
    for core, ref in ((0, quad_ref), (1, other_ref)):
        for yh, step in [(yh, step) for yh in range(2) for step in range(4)]:
            block = (
                (place_ref[0] ^ yh) * 8 + (place_ref[1] ^ step) * 2 + (place_ref[2] ^ core)
            )
            full_ref[pl.ds(pl.multiple_of(block * 96, 96), 96), :] = ref[step, yh]

    def project(step, carry):
        row = pl.multiple_of(step * 256, 256)
        part = jnp.dot(
            normed_ref[pl.ds(row, 256), :], full_ref[...], preferred_element_type=F32
        ) + bias_ref[...]
        part = part.astype(BF16).astype(F32).reshape(4, 64, width)
        field[pl.ds(step * 4, 4), :, 0:width] = part
        return carry

    lax.fori_loop(0, 4, project, 0)
    sums[...] = jnp.zeros_like(sums)
    tiles = padded // 128

    def pairs(step, carry):
        row = pl.multiple_of((step // tiles) * 8, 8)
        lane = pl.multiple_of((step % tiles) * 128, 128)
        here = (pl.ds(row, 8), pl.ds(lane, 128))
        values = [field[m, here[0], here[1]] for m in range(count)]
        total = [None] * count
        for m in range(count):
            for k in range(m + 1, count):
                s = slope(values[m] - values[k])
                total[m] = s if total[m] is None else total[m] + s
                total[k] = -s if total[k] is None else total[k] - s
        true = truth_ref[here[0], here[1]]
        scale = wt_ref[0:1, pl.ds(lane, 128)]
        column = None
        for m in range(count):
            value = scale * (slope(values[m] - true) * (1.0 / count) - coef * total[m])
            value = value.astype(BF16).astype(F32)
            field[m, here[0], here[1]] = value
            column = value if column is None else column + value
        sums[:, pl.ds(lane, 128)] += column
        return carry

    lax.fori_loop(0, 8 * tiles, pairs, 0)
    bias_out_ref[...] = jnp.sum(sums[...], axis=0, keepdims=True)

    def store(step, carry):
        dfield_ref[step] = field[pl.ds(step * 2, 2), :, 0:width].astype(BF16)
        return carry

    lax.fori_loop(0, count // 2, store, 0)


def grad_kernel(place_ref, dfield_ref, full_ref, bias_part_ref, gain_ref, *refs):
    pieces = refs[:8]
    keep_ref, send_ref, small_ref, flipped_ref, grad, rows = refs[8:]
    for k in range(8):
        flipped_ref[:, pl.ds(128 * k, 128)] = pieces[k][...]
    width = full_ref.shape[1]
    features = full_ref.shape[0]

    def weight_grad(step, carry):
        row = pl.multiple_of(step * 512, 512)
        grad[pl.ds(row, 512), :] = jnp.dot(
            flipped_ref[pl.ds(row, 512), :], dfield_ref[...], preferred_element_type=F32
        )
        return carry

    lax.fori_loop(0, features // 512, weight_grad, 0)

    def gain_part(step, carry):
        row = pl.multiple_of(step * 128, 128)
        part = jnp.sum(
            grad[pl.ds(row, 128), :] * full_ref[pl.ds(row, 128), :].astype(F32),
            axis=1, keepdims=True,
        )
        rows[:, pl.ds(row, 128)] = jnp.broadcast_to(part, (128, 128)).T[0:8]
        return carry

    lax.fori_loop(0, features // 128, gain_part, 0)
    small_ref[...] = jnp.zeros_like(small_ref)
    for n in range(3):
        cut = slice(512 * n, 512 * (n + 1))
        small_ref[n : n + 1, :] = rows[0:1, cut] / gain_ref[:, cut]
        stop = min(512 * (n + 1), width)
        small_ref[3 + n : 4 + n, 0 : stop - 512 * n] = bias_part_ref[:, 512 * n : stop]
    small = small_ref[...]
    high = small.astype(BF16)
    low = (small - high.astype(F32)).astype(BF16)
    send_ref[0:16, :] = jnp.zeros((16, width), BF16)
    send_ref[0:16, 0:512] = jnp.concatenate([high, low], axis=0)
    for yh in range(2):
        for step in range(4):
            base = (place_ref[0] ^ yh) * 8 + (place_ref[1] ^ step) * 2
            mine = pl.multiple_of((base + place_ref[2]) * 96, 96)
            other = pl.multiple_of((base + (place_ref[2] ^ 1)) * 96, 96)
            keep_ref[yh, step] = grad[pl.ds(mine, 96), :]
            start = 16 + 96 * (yh * 4 + step)
            send_ref[start : start + 96, :] = grad[pl.ds(other, 96), :].astype(BF16)


def backward_kernel(place_ref, tokens_ref, gain_ref, full_ref, *refs):
    pieces, out_ref, dfield, grad = refs[:8], refs[8], refs[9], refs[10]
    features = full_ref.shape[0]
    for k in range(8):
        dfield[pl.ds(128 * k, 128), :] = pieces[k][...].reshape(128, -1)

    def matmul(step, carry):
        lane = pl.multiple_of(step * 256, 256)
        grad[:, pl.ds(lane, 256)] = lax.dot_general(
            dfield[...], full_ref[pl.ds(lane, 256), :], (((1,), (1,)), ((), ())),
            preferred_element_type=F32,
        )
        return carry

    lax.fori_loop(0, features // 256, matmul, 0)

    def rows(step, carry):
        k, m = step // 2, step % 2
        j = place_ref[3] ^ k
        wide = tokens_ref[m, j].astype(F32)
        mean = jnp.mean(wide, -1, keepdims=True)
        centred = wide - mean
        variance = jnp.mean(centred * centred, -1, keepdims=True)
        inverse = lax.rsqrt(variance + EPS)
        xhat = centred * inverse
        scaled = grad[pl.ds(pl.multiple_of(step * 64, 64), 64), :] * gain_ref[...]
        out = inverse * (
            scaled
            - jnp.mean(scaled, -1, keepdims=True)
            - xhat * jnp.mean(scaled * xhat, -1, keepdims=True)
        )
        out_ref[m, j] = out.astype(BF16)
        return carry

    lax.fori_loop(0, 16, rows, 0)


def member_rows(parts, where):
    _, _, rows, width = parts.shape
    members = 8 * rows
    index = jnp.arange(members)
    block, inside = index // rows, index % rows
    source = (((block % 2) ^ where["yl"]) * 4 + ((block // 2) ^ where["x"])) * rows + inside
    pick = (source[:, None] == jnp.arange(members)[None, :]).astype(BF16)
    return jnp.dot(
        pick, parts.reshape(members, width), preferred_element_type=F32
    ).astype(BF16)


def pack(small, width):
    high = lax.reduce_precision(small, 8, 7)
    both = jnp.concatenate([high, small - high], axis=0).astype(BF16)
    return jnp.pad(both, ((0, 0), (0, width - both.shape[1])))


def unpack(rows):
    rows = rows[:, :512].astype(F32)
    return rows[:8] + rows[8:16]


def on_device(tokens, gain, weight, bias, target, channel_weight):
    where = {axis: lax.axis_index(axis) for axis in SIZE}
    member = where["x"] * 2 + where["yl"]
    space = (where["yh"] * 4 + where["z"]) * 2 + where["core"]
    place = jnp.stack([where["yh"], where["z"], where["core"], member]).astype(jnp.int32)
    smem = pl.BlockSpec(memory_space=pltpu.SMEM)
    features = tokens.shape[-1]
    outs = weight.shape[1]
    padded = -(-outs // 128) * 128
    gain_row = gain.reshape(1, features)

    pieces = tokens.reshape(2, 8, 64, features)
    sources = [
        lax.dynamic_index_in_dim(pieces, member ^ k, 1, keepdims=False) for k in range(8)
    ]
    arrived = {0: sources[0], 1: swap_member(sources[1], 1), 4: swap_member(sources[4], 4)}
    near = jnp.stack([weight] + [swap(weight, "x", k) for k in (1, 2, 3)])
    (p3, p6), (near,) = after((sources[3], sources[6]), near)
    arrived[3], arrived[6] = swap_member(p3, 3), swap_member(p6, 6)
    rows_y = [near] + [swap_y(near, k) for k in (1, 2, 3)]
    pair = jnp.stack(
        [
            member_rows(jnp.stack(rows_y[0:2]), where),
            member_rows(jnp.stack(rows_y[2:4]), where),
        ]
    )
    (pair, p7, p2, p5), (arrived[1], arrived[4]) = after(
        (pair, sources[7], sources[2], sources[5]), arrived[1], arrived[4]
    )
    for k, piece in ((7, p7), (2, p2), (5, p5)):
        arrived[k] = swap_member(piece, k)
    quad = jnp.stack([pair] + [swap(pair, "z", k) for k in (1, 2, 3)])
    late = (3, 6, 7, 2, 5)
    (quad,), done = after((quad,), *[arrived[k] for k in late])
    for k, piece in zip(late, done):
        arrived[k] = piece
    other = swap(quad, "core", 1)
    normed = [norm_piece(arrived[k], gain_row) for k in range(8)]

    t_here, l_here = member // 4, member % 4
    image = lax.dynamic_slice(
        target, (0, 4 * t_here, 256 * l_here), (target.shape[0], 4, 256)
    ).reshape(-1, 256)
    truth = pl.pallas_call(
        truth_kernel,
        out_shape=jax.ShapeDtypeStruct((64, padded), F32),
        in_specs=vmem(1),
        out_specs=vmem(1)[0],
        compiler_params=params(8),
        cost_estimate=cost(2000000000, 8000000),
        name="truth",
    )(image)
    table = jnp.asarray(latitude_weights(128).reshape(32, 4))
    latw = lax.dynamic_index_in_dim(table, space * 2 + t_here, 0, keepdims=False)
    wt = jnp.broadcast_to(
        channel_weight[:, None, None] * latw[None, :, None], (channel_weight.shape[0], 4, 4)
    ).reshape(1, outs)
    wt = jnp.pad(wt, ((0, 0), (0, padded - outs)))

    full, dfield, bias_part = pl.pallas_call(
        pairs_kernel,
        out_shape=(
            jax.ShapeDtypeStruct((features, outs), BF16),
            jax.ShapeDtypeStruct((8, 2, 64, outs), BF16),
            jax.ShapeDtypeStruct((1, padded), F32),
        ),
        in_specs=[smem] + vmem(13),
        out_specs=tuple(vmem(3)),
        scratch_shapes=[
            pltpu.VMEM((1024, features), BF16),
            pltpu.VMEM((16, 64, padded), F32),
            pltpu.VMEM((8, padded), F32),
        ],
        compiler_params=params(32),
        cost_estimate=cost(20000000000, 80000000),
        name="pairs",
    )(place, quad, other, bias.reshape(1, outs), truth, wt, *[n[0] for n in normed])

    returned = {0: dfield[0], 1: swap_member(dfield[1], 1), 3: swap_member(dfield[3], 3)}
    keep, send, small = pl.pallas_call(
        grad_kernel,
        out_shape=(
            jax.ShapeDtypeStruct((2, 4, 96, outs), F32),
            jax.ShapeDtypeStruct((16 + 768, outs), BF16),
            jax.ShapeDtypeStruct((8, 512), F32),
        ),
        in_specs=[smem] + vmem(12),
        out_specs=tuple(vmem(3)),
        scratch_shapes=[
            pltpu.VMEM((features, 1024), BF16),
            pltpu.VMEM((features, outs), F32),
            pltpu.VMEM((8, features), F32),
        ],
        compiler_params=params(32),
        cost_estimate=cost(12000000000, 45000000),
        name="weight_gradient",
    )(
        place, dfield.reshape(1024, outs), full, bias_part, gain_row,
        *[n[1] for n in normed],
    )

    def pick(value, index):
        return lax.dynamic_index_in_dim(value, index, 0, keepdims=False)

    def spread(mine, blocks, small, moves):
        came = [
            move(jnp.concatenate([pack(small, outs), block.astype(BF16)], axis=0))
            for move, block in zip(moves, blocks)
        ]
        return (
            sum([c[16:].astype(F32) for c in came], mine),
            sum([unpack(c) for c in came], small),
        )

    rest = (6, 4, 5, 7, 2)
    (send, *held), (returned[1], returned[3]) = after(
        (send, *[dfield[k] for k in rest]), returned[1], returned[3]
    )
    for k, piece in zip(rest, held):
        returned[k] = swap_member(piece, k)
    came = swap(send, "core", 1)
    total = keep + came[16:].reshape(keep.shape).astype(F32)
    small = small + unpack(came)
    total, small = spread(
        total[:, 0].reshape(-1, outs),
        [total[:, k].reshape(-1, outs) for k in (1, 2, 3)],
        small,
        [functools.partial(swap, axis="z", step=k) for k in (1, 2, 3)],
    )
    result = pl.pallas_call(
        backward_kernel,
        out_shape=jax.ShapeDtypeStruct((2, 8, 64, features), BF16),
        in_specs=[smem] + vmem(11),
        out_specs=vmem(1)[0],
        scratch_shapes=[pltpu.VMEM((1024, outs), BF16), pltpu.VMEM((1024, features), F32)],
        compiler_params=params(32),
        cost_estimate=cost(16000000000, 60000000),
        name="backward",
    )(place, pieces, gain_row, full, *[returned[k] for k in range(8)])
    (total, small), (result,) = after((total, small), result)
    total = total.reshape(2, 4, 2, 12, outs)

    def slab(step):
        block = pick(total[step // 2].transpose(1, 0, 2, 3), where["yl"] ^ (step % 2))
        return block.reshape(48, outs)

    total, small = spread(
        slab(0),
        [slab(k) for k in (1, 2, 3)],
        small,
        [functools.partial(swap_y, step=k) for k in (1, 2, 3)],
    )
    total = total.reshape(4, 12, outs)
    share, small = spread(
        pick(total, where["x"]),
        [pick(total, where["x"] ^ k) for k in (1, 2, 3)],
        small,
        [functools.partial(swap, axis="x", step=k) for k in (1, 2, 3)],
    )
    return (
        result.reshape(tokens.shape),
        small[0:3].reshape(-1),
        share,
        small[3:6].reshape(-1)[:outs],
    )


def solution(mesh):
    fine = Mesh(
        mesh.devices.reshape(2, 4, 2, 4, 2), ("yh", "z", "core", "x", "yl")
    )
    both = SPACE + MEMBER
    return jax.shard_map(
        on_device,
        mesh=fine,
        in_specs=(
            P(MEMBER, SPACE, None, None),
            P(),
            P(both, None),
            P(),
            P(None, SPACE, None),
            P(),
        ),
        out_specs=(P(MEMBER, SPACE, None, None), P(), P(both, None), P()),
        check_vma=False,
    )
```

```python
import functools

import jax
import jax.numpy as jnp
import numpy as np
from jax import lax
from jax.experimental import pallas as pl
from jax.experimental.pallas import tpu as pltpu
from jax.sharding import Mesh
from jax.sharding import PartitionSpec as P

ALPHA = 0.95
DELTA = 0.1
EPS = 1e-05
SIZE = dict(yh=2, z=4, core=2, x=4, yl=2)
SPACE = ("yh", "z", "core")
MEMBER = ("x", "yl")
BF16 = jnp.bfloat16
FIRST, SECOND = (0, 1, 4, 5), (3, 6, 7, 2)
F32 = jnp.float32


def params(mebibytes):
    return pltpu.CompilerParams(vmem_limit_bytes=mebibytes * 1024 * 1024)


def cost(flops, bytes_accessed):
    return pl.CostEstimate(flops=flops, bytes_accessed=bytes_accessed, transcendentals=0)


def after(values, *done):
    out = lax.optimization_barrier((*values, *done))
    return out[: len(values)], out[len(values) :]


def latitude_weights(rows):
    index = np.arange(rows, dtype=np.float64)
    cosine = np.cos((60.0 - 0.25 * (index + 0.5)) * (np.pi / 180.0))
    return (cosine / cosine.mean()).astype(np.float32)


def swap(value, axis, step):
    return lax.ppermute(value, axis, [(i, i ^ step) for i in range(SIZE[axis])])


def swap_y(value, step):
    return lax.ppermute(value, ("yh", "yl"), [(i, i ^ step) for i in range(4)])


def swap_member(value, step):
    return lax.ppermute(value, MEMBER, [(i, i ^ step) for i in range(8)])


def vmem(count):
    return [pl.BlockSpec(memory_space=pltpu.VMEM)] * count


def truth_kernel(image_ref, out_ref):
    image = image_ref[...]
    chan_rows, cols = image.shape
    cells = cols // 4
    total = jnp.zeros(out_ref.shape, F32)
    for q in range(4):
        pick = (
            lax.broadcasted_iota(jnp.int32, (cells, cols), 1)
            == 4 * lax.broadcasted_iota(jnp.int32, (cells, cols), 0) + q
        ).astype(BF16)
        part = lax.dot_general(
            pick, image, (((1,), (1,)), ((), ())), preferred_element_type=F32
        ).astype(BF16)
        place = (
            lax.broadcasted_iota(jnp.int32, (chan_rows, total.shape[1]), 1)
            == 4 * lax.broadcasted_iota(jnp.int32, (chan_rows, total.shape[1]), 0) + q
        ).astype(BF16)
        total = total + jnp.dot(part, place, preferred_element_type=F32)
    out_ref[...] = total


def norm_kernel(tokens_ref, gain_ref, normed_ref, flipped_ref):
    wide = tokens_ref[...].astype(F32)
    mean = jnp.mean(wide, -1, keepdims=True)
    centred = wide - mean
    variance = jnp.mean(centred * centred, -1, keepdims=True)
    normed = (centred * lax.rsqrt(variance + EPS) * gain_ref[...]).astype(BF16)
    normed_ref[...] = normed
    flipped_ref[...] = normed.T


def norm_piece(piece, gain_row):
    features = piece.shape[-1]
    return pl.pallas_call(
        norm_kernel,
        out_shape=(
            jax.ShapeDtypeStruct((128, features), BF16),
            jax.ShapeDtypeStruct((features, 128), BF16),
        ),
        in_specs=vmem(2),
        out_specs=tuple(vmem(2)),
        compiler_params=params(8),
        cost_estimate=cost(2000000000, 8000000),
        name="norm",
    )(piece.reshape(128, features), gain_row)


def slope(value):
    return value * lax.rsqrt(value * value + DELTA * DELTA)


def pairs_kernel(
    place_ref, quad_ref, other_ref, bias_ref, truth_ref, wt_ref, *refs
):
    pieces = refs[:8]
    full_ref, bias_out_ref, *dfield_refs = refs[8:18]
    normed_ref, field, sums = refs[18:]
    for k in range(8):
        normed_ref[pl.ds(128 * k, 128), :] = pieces[k][...]
    width = full_ref.shape[1]
    padded = field.shape[2]
    count = 16
    coef = (1.0 - (1.0 - ALPHA) / count) / (count * (count - 1))
    for core, ref in ((0, quad_ref), (1, other_ref)):
        for yh, step in [(yh, step) for yh in range(2) for step in range(4)]:
            block = (
                (place_ref[0] ^ yh) * 8 + (place_ref[1] ^ step) * 2 + (place_ref[2] ^ core)
            )
            full_ref[pl.ds(pl.multiple_of(block * 96, 96), 96), :] = ref[step, yh]

    def project(step, carry):
        row = pl.multiple_of(step * 256, 256)
        part = jnp.dot(
            normed_ref[pl.ds(row, 256), :], full_ref[...], preferred_element_type=F32
        ) + bias_ref[...]
        part = part.astype(BF16).astype(F32).reshape(4, 64, width)
        field[pl.ds(step * 4, 4), :, 0:width] = part
        return carry

    lax.fori_loop(0, 4, project, 0)
    sums[...] = jnp.zeros_like(sums)
    tiles = padded // 128

    def pairs(step, carry):
        row = pl.multiple_of((step // tiles) * 8, 8)
        lane = pl.multiple_of((step % tiles) * 128, 128)
        here = (pl.ds(row, 8), pl.ds(lane, 128))
        values = [field[m, here[0], here[1]] for m in range(count)]
        total = [None] * count
        for m in range(count):
            for k in range(m + 1, count):
                s = slope(values[m] - values[k])
                total[m] = s if total[m] is None else total[m] + s
                total[k] = -s if total[k] is None else total[k] - s
        true = truth_ref[here[0], here[1]]
        scale = wt_ref[0:1, pl.ds(lane, 128)]
        column = None
        for m in range(count):
            value = scale * (slope(values[m] - true) * (1.0 / count) - coef * total[m])
            value = value.astype(BF16).astype(F32)
            field[m, here[0], here[1]] = value
            column = value if column is None else column + value
        sums[:, pl.ds(lane, 128)] += column
        return carry

    lax.fori_loop(0, 8 * tiles, pairs, 0)
    bias_out_ref[...] = jnp.sum(sums[...], axis=0, keepdims=True)

    for k in range(8):
        for m in range(2):
            dfield_refs[k][64 * m : 64 * m + 64, :] = field[2 * k + m, :, 0:width].astype(BF16)


def grad_kernel(place_ref, full_ref, bias_part_ref, gain_ref, *refs):
    pieces, fields = refs[:8], refs[8:16]
    keep_ref, send_ref, small_ref, flipped_ref, dfield_ref, grad, rows = refs[16:]
    for k in range(8):
        flipped_ref[:, pl.ds(128 * k, 128)] = pieces[k][...]
        dfield_ref[pl.ds(128 * k, 128), :] = fields[k][...]
    width = full_ref.shape[1]
    features = full_ref.shape[0]

    def weight_grad(step, carry):
        row = pl.multiple_of(step * 512, 512)
        grad[pl.ds(row, 512), :] = jnp.dot(
            flipped_ref[pl.ds(row, 512), :], dfield_ref[...], preferred_element_type=F32
        )
        return carry

    lax.fori_loop(0, features // 512, weight_grad, 0)

    def gain_part(step, carry):
        row = pl.multiple_of(step * 128, 128)
        part = jnp.sum(
            grad[pl.ds(row, 128), :] * full_ref[pl.ds(row, 128), :].astype(F32),
            axis=1, keepdims=True,
        )
        rows[:, pl.ds(row, 128)] = jnp.broadcast_to(part, (128, 128)).T[0:8]
        return carry

    lax.fori_loop(0, features // 128, gain_part, 0)
    small_ref[...] = jnp.zeros_like(small_ref)
    for n in range(3):
        cut = slice(512 * n, 512 * (n + 1))
        small_ref[n : n + 1, :] = rows[0:1, cut] / gain_ref[:, cut]
        stop = min(512 * (n + 1), width)
        small_ref[3 + n : 4 + n, 0 : stop - 512 * n] = bias_part_ref[:, 512 * n : stop]
    put_small(send_ref, small_ref[...])
    for yh in range(2):
        for step in range(4):
            base = (place_ref[0] ^ yh) * 8 + (place_ref[1] ^ step) * 2
            mine = pl.multiple_of((base + place_ref[2]) * 96, 96)
            other = pl.multiple_of((base + (place_ref[2] ^ 1)) * 96, 96)
            keep_ref[yh, step] = grad[pl.ds(mine, 96), :]
            start = 16 + 96 * (yh * 4 + step)
            send_ref[start : start + 96, :] = grad[pl.ds(other, 96), :].astype(BF16)


def backward_kernel(order, before, place_ref, tokens_ref, gain_ref, full_ref, *refs):
    count = len(order)
    earlier, pieces = refs[:before], refs[before : before + count]
    out_ref, dfield, grad = refs[before + count :]
    features = full_ref.shape[0]
    for n in range(count):
        dfield[pl.ds(128 * n, 128), :] = pieces[n][...].reshape(128, -1)

    def matmul(step, carry):
        lane = pl.multiple_of(step * 256, 256)
        grad[:, pl.ds(lane, 256)] = lax.dot_general(
            dfield[...], full_ref[pl.ds(lane, 256), :], (((1,), (1,)), ((), ())),
            preferred_element_type=F32,
        )
        return carry

    lax.fori_loop(0, features // 256, matmul, 0)
    for n, k in enumerate(order):
        j = place_ref[3] ^ k

        def rows(m, carry, n=n, j=j):
            wide = tokens_ref[m, j].astype(F32)
            mean = jnp.mean(wide, -1, keepdims=True)
            centred = wide - mean
            variance = jnp.mean(centred * centred, -1, keepdims=True)
            inverse = lax.rsqrt(variance + EPS)
            xhat = centred * inverse
            start = pl.multiple_of(128 * n + m * 64, 64)
            scaled = grad[pl.ds(start, 64), :] * gain_ref[...]
            out = inverse * (
                scaled
                - jnp.mean(scaled, -1, keepdims=True)
                - xhat * jnp.mean(scaled * xhat, -1, keepdims=True)
            )
            if before:
                out_ref[m, j] = out.astype(BF16)
            else:
                out_ref[n, m] = out.astype(BF16)
            return carry

        lax.fori_loop(0, 2, rows, 0)
    if before:
        for n, k in enumerate(FIRST):
            for m in range(2):
                out_ref[m, place_ref[3] ^ k] = earlier[0][n, m]


def member_rows(parts, where):
    _, _, rows, width = parts.shape
    members = 8 * rows
    index = jnp.arange(members)
    block, inside = index // rows, index % rows
    source = (((block // 2) ^ where["x"]) * 2 + ((block % 2) ^ where["yl"])) * rows + inside
    pick = (source[:, None] == jnp.arange(members)[None, :]).astype(BF16)
    return jnp.dot(
        pick, parts.reshape(members, width), preferred_element_type=F32
    ).astype(BF16)


def put_small(ref, small):
    high = small.astype(BF16)
    low = (small - high.astype(F32)).astype(BF16)
    ref[0:16, :] = jnp.zeros((16, ref.shape[1]), BF16)
    ref[0:16, 0:512] = jnp.concatenate([high, low], axis=0)


def get_small(ref):
    rows = ref[0:16, 0:512].astype(F32)
    return rows[0:8] + rows[8:16]


def rows_of(picked, values):
    high = values.astype(BF16)
    low = (values - high.astype(F32)).astype(BF16)
    picked = picked.astype(BF16)
    return jnp.dot(picked, high, preferred_element_type=F32), jnp.dot(
        picked, low, preferred_element_type=F32
    )


def core_kernel(keep_ref, small_ref, came_ref, own_ref, small_out_ref, *sends):
    small = small_ref[...] + get_small(came_ref)
    small_out_ref[...] = small
    for step in range(4):
        for yh in range(2):
            start = 16 + 96 * (yh * 4 + step)
            block = keep_ref[yh, step] + came_ref[start : start + 96, :].astype(F32)
            if step == 0:
                own_ref[96 * yh : 96 * yh + 96, :] = block
            else:
                sends[step - 1][16 + 96 * yh : 112 + 96 * yh, :] = block.astype(BF16)
    for ref in sends:
        put_small(ref, small)


def iota(shape, axis):
    return lax.broadcasted_iota(jnp.int32, shape, axis)


def gather_sums(own_ref, small_ref, came):
    total, small = own_ref[...], small_ref[...]
    for ref in came:
        total = total + ref[16 : 16 + own_ref.shape[0], :].astype(F32)
        small = small + get_small(ref)
    return total, small


def z_kernel(place_ref, own_ref, small_ref, a_ref, b_ref, c_ref, own_out_ref, small_out_ref, *sends):
    total, small = gather_sums(own_ref, small_ref, (a_ref, b_ref, c_ref))
    small_out_ref[...] = small
    row, source = iota((48, 192), 0), iota((48, 192), 1)
    for step in range(4):
        yl = place_ref[5] ^ (step % 2)
        wanted = (step // 2) * 96 + (row // 12) * 24 + yl * 12 + row % 12
        high, low = rows_of(source == wanted, total)
        if step == 0:
            own_out_ref[...] = high + low
        else:
            sends[step - 1][16:64, :] = high.astype(BF16)
            put_small(sends[step - 1], small)


def y_kernel(place_ref, own_ref, small_ref, a_ref, b_ref, c_ref, own_out_ref, small_out_ref, *sends):
    total, small = gather_sums(own_ref, small_ref, (a_ref, b_ref, c_ref))
    small_out_ref[...] = small
    row, source = iota((16, 48), 0), iota((16, 48), 1)
    for step in range(4):
        wanted = (place_ref[4] ^ step) * 12 + row
        high, low = rows_of((source == wanted) & (row < 12), total)
        if step == 0:
            own_out_ref[...] = high + low
        else:
            sends[step - 1][16:32, :] = high.astype(BF16)
            put_small(sends[step - 1], small)


def x_kernel(own_ref, small_ref, a_ref, b_ref, c_ref, share_ref, small_out_ref):
    total, small = gather_sums(own_ref, small_ref, (a_ref, b_ref, c_ref))
    share_ref[...] = total[0:12]
    small_out_ref[...] = small


def on_device(tokens, gain, weight, bias, target, channel_weight):
    where = {axis: lax.axis_index(axis) for axis in SIZE}
    member = where["x"] * 2 + where["yl"]
    space = (where["yh"] * 4 + where["z"]) * 2 + where["core"]
    place = jnp.stack(
        [where["yh"], where["z"], where["core"], member, where["x"], where["yl"]]
    ).astype(jnp.int32)
    smem = pl.BlockSpec(memory_space=pltpu.SMEM)
    features = tokens.shape[-1]
    outs = weight.shape[1]
    padded = -(-outs // 128) * 128
    gain_row = gain.reshape(1, features)

    pieces = tokens.reshape(2, 8, 64, features)
    sources = [
        lax.dynamic_index_in_dim(pieces, member ^ k, 1, keepdims=False) for k in range(8)
    ]
    t_here, l_here = member // 4, member % 4
    image = lax.dynamic_slice(
        target, (0, 4 * t_here, 256 * l_here), (target.shape[0], 4, 256)
    ).reshape(-1, 256)
    truth = pl.pallas_call(
        truth_kernel,
        out_shape=jax.ShapeDtypeStruct((64, padded), F32),
        in_specs=vmem(1),
        out_specs=vmem(1)[0],
        compiler_params=params(8),
        cost_estimate=cost(2000000000, 8000000),
        name="truth",
    )(image)
    table = jnp.asarray(latitude_weights(128).reshape(32, 4))
    latw = lax.dynamic_index_in_dim(table, space * 2 + t_here, 0, keepdims=False)
    wt = jnp.broadcast_to(
        channel_weight[:, None, None] * latw[None, :, None], (channel_weight.shape[0], 4, 4)
    ).reshape(1, outs)
    wt = jnp.pad(wt, ((0, 0), (0, padded - outs)))

    arrived = {0: sources[0], 4: swap_member(sources[4], 4)}
    near = jnp.stack([weight] + [swap_y(weight, k) for k in (1, 2, 3)])
    (p1, p2), (near,) = after((sources[1], sources[2]), near)
    wide = jnp.stack([near] + [swap(near, "x", k) for k in (1, 2, 3)])
    arrived[1], arrived[2] = swap_member(p1, 1), swap_member(p2, 2)
    pair = jnp.stack([member_rows(wide[:, 2 * k : 2 * k + 2], where) for k in range(2)])
    (pair, p3, p6), done = after(
        (pair, sources[3], sources[6]), arrived[4], arrived[1], arrived[2], truth, wt
    )
    arrived[4], arrived[1], arrived[2], truth, wt = done
    quad = jnp.stack([pair] + [swap(pair, "z", k) for k in (1, 2, 3)])
    arrived[3], arrived[6] = swap_member(p3, 3), swap_member(p6, 6)
    (p7, p5), (arrived[3], arrived[6]) = after(
        (sources[7], sources[5]), arrived[3], arrived[6]
    )
    arrived[7], arrived[5] = swap_member(p7, 7), swap_member(p5, 5)
    normed = {k: norm_piece(arrived[k], gain_row) for k in (0, 4, 1, 2, 3, 6)}
    early = [n for k in (0, 4, 1, 2, 3, 6) for n in normed[k]]
    (quad,), done = after((quad,), arrived[7], *early)
    arrived[7] = done[0]
    for n, k in enumerate((0, 4, 1, 2, 3, 6)):
        normed[k] = done[1 + 2 * n : 3 + 2 * n]
    other = swap(quad, "core", 1)
    for k in (7, 5):
        normed[k] = norm_piece(arrived[k], gain_row)

    full, bias_part, *dfield = pl.pallas_call(
        pairs_kernel,
        out_shape=(
            jax.ShapeDtypeStruct((features, outs), BF16),
            jax.ShapeDtypeStruct((1, padded), F32),
        )
        + (jax.ShapeDtypeStruct((128, outs), BF16),) * 8,
        in_specs=[smem] + vmem(13),
        out_specs=tuple(vmem(10)),
        scratch_shapes=[
            pltpu.VMEM((1024, features), BF16),
            pltpu.VMEM((16, 64, padded), F32),
            pltpu.VMEM((8, padded), F32),
        ],
        compiler_params=params(32),
        cost_estimate=cost(20000000000, 80000000),
        name="pairs",
    )(place, quad, other, bias.reshape(1, outs), truth, wt, *[normed[k][0] for k in range(8)])

    returned = {0: dfield[0]}
    for k in (1, 4, 5):
        returned[k] = swap_member(dfield[k], k)
    keep, send, small = pl.pallas_call(
        grad_kernel,
        out_shape=(
            jax.ShapeDtypeStruct((2, 4, 96, outs), F32),
            jax.ShapeDtypeStruct((16 + 768, outs), BF16),
            jax.ShapeDtypeStruct((8, 512), F32),
        ),
        in_specs=[smem] + vmem(19),
        out_specs=tuple(vmem(3)),
        scratch_shapes=[
            pltpu.VMEM((features, 1024), BF16),
            pltpu.VMEM((1024, outs), BF16),
            pltpu.VMEM((features, outs), F32),
            pltpu.VMEM((8, features), F32),
        ],
        compiler_params=params(34),
        cost_estimate=cost(12000000000, 45000000),
        name="weight_gradient",
    )(
        place, full, bias_part, gain_row,
        *[normed[k][1] for k in range(8)], *dfield,
    )

    def backward(order, before):
        count = len(order)
        return pl.pallas_call(
            functools.partial(backward_kernel, order, len(before)),
            out_shape=jax.ShapeDtypeStruct(
                (2, 8, 64, features) if before else (count, 2, 64, features), BF16
            ),
            in_specs=[smem] + vmem(3 + count + len(before)),
            out_specs=vmem(1)[0],
            scratch_shapes=[
                pltpu.VMEM((128 * count, outs), BF16),
                pltpu.VMEM((128 * count, features), F32),
            ],
            compiler_params=params(32),
            cost_estimate=cost(8000000000, 30000000),
            name="backward",
        )(place, pieces, gain_row, full, *before, *[returned[k] for k in order])

    def combine(kernel, name, own_rows, send_rows, sends, *operands):
        return pl.pallas_call(
            kernel,
            out_shape=(
                jax.ShapeDtypeStruct((own_rows, outs), F32),
                jax.ShapeDtypeStruct((8, 512), F32),
            )
            + (jax.ShapeDtypeStruct((send_rows, outs), BF16),) * sends,
            in_specs=([smem] if operands[0] is place else [])
            + vmem(len(operands) - (operands[0] is place)),
            out_specs=tuple(vmem(2 + sends)),
            compiler_params=params(16),
            cost_estimate=cost(1000000000, 4000000),
            name=name,
        )(*operands)

    (send,), done = after((send,), returned[1], returned[4], returned[5])
    returned[1], returned[4], returned[5] = done
    came = swap(send, "core", 1)
    own, small, *sends = combine(core_kernel, "core_sums", 192, 208, 3, keep, small, came)
    sends[0], sends[1], sends[2], d3, d6 = after(
        (*sends, dfield[3], dfield[6])
    )[0]
    came = [swap(value, "z", k) for k, value in zip((1, 2, 3), sends)]
    returned[3], returned[6] = swap_member(d3, 3), swap_member(d6, 6)
    half = backward(FIRST, ())
    (d7, d2), (half, returned[3], returned[6]) = after(
        (dfield[7], dfield[2]), half, returned[3], returned[6]
    )
    returned[7], returned[2] = swap_member(d7, 7), swap_member(d2, 2)
    came, (half, returned[7], returned[2]) = after(
        came, half, returned[7], returned[2]
    )
    own, small, *sends = combine(z_kernel, "z_sums", 48, 64, 3, place, own, small, *came)
    came = [swap_y(value, k) for k, value in zip((1, 2, 3), sends)]
    result = backward(SECOND, (half,))
    came, (result,) = after(came, result)
    own, small, *sends = combine(y_kernel, "y_sums", 16, 32, 3, place, own, small, *came)
    came = [swap(value, "x", k) for k, value in zip((1, 2, 3), sends)]
    share, small = combine(x_kernel, "x_sums", 12, 0, 0, own, small, *came)
    return (
        result.reshape(tokens.shape),
        small[0:3].reshape(-1),
        share,
        small[3:6].reshape(-1)[:outs],
    )


def solution(mesh):
    fine = Mesh(
        mesh.devices.reshape(2, 4, 2, 4, 2), ("yh", "z", "core", "x", "yl")
    )
    both = SPACE + MEMBER
    return jax.shard_map(
        on_device,
        mesh=fine,
        in_specs=(
            P(MEMBER, SPACE, None, None),
            P(),
            P(both, None),
            P(),
            P(None, SPACE, None),
            P(),
        ),
        out_specs=(P(MEMBER, SPACE, None, None), P(), P(both, None), P()),
        check_vma=False,
    )
```

```python
import functools

import jax
import jax.numpy as jnp
import numpy as np
from jax import lax
from jax.experimental import pallas as pl
from jax.experimental.pallas import tpu as pltpu
from jax.sharding import Mesh
from jax.sharding import PartitionSpec as P

ALPHA = 0.95
DELTA = 0.1
EPS = 1e-05
SIZE = dict(yh=2, z=4, core=2, x=4, yl=2)
SPACE = ("yh", "z", "core")
MEMBER = ("x", "yl")
BF16 = jnp.bfloat16
FIRST, SECOND = (0, 1, 4), (3, 6, 7, 2, 5)
F32 = jnp.float32


def params(mebibytes):
    return pltpu.CompilerParams(vmem_limit_bytes=mebibytes * 1024 * 1024)


def cost(flops, bytes_accessed):
    return pl.CostEstimate(flops=flops, bytes_accessed=bytes_accessed, transcendentals=0)


def after(values, *done):
    out = lax.optimization_barrier((*values, *done))
    return out[: len(values)], out[len(values) :]


def latitude_weights(rows):
    index = np.arange(rows, dtype=np.float64)
    cosine = np.cos((60.0 - 0.25 * (index + 0.5)) * (np.pi / 180.0))
    return (cosine / cosine.mean()).astype(np.float32)


def swap(value, axis, step):
    return lax.ppermute(value, axis, [(i, i ^ step) for i in range(SIZE[axis])])


def swap_y(value, step):
    return lax.ppermute(value, ("yh", "yl"), [(i, i ^ step) for i in range(4)])


def swap_member(value, step):
    return lax.ppermute(value, MEMBER, [(i, i ^ step) for i in range(8)])


def vmem(count):
    return [pl.BlockSpec(memory_space=pltpu.VMEM)] * count


def truth_kernel(image_ref, out_ref):
    image = image_ref[...]
    chan_rows, cols = image.shape
    cells = cols // 4
    total = jnp.zeros(out_ref.shape, F32)
    for q in range(4):
        pick = (
            lax.broadcasted_iota(jnp.int32, (cells, cols), 1)
            == 4 * lax.broadcasted_iota(jnp.int32, (cells, cols), 0) + q
        ).astype(BF16)
        part = lax.dot_general(
            pick, image, (((1,), (1,)), ((), ())), preferred_element_type=F32
        ).astype(BF16)
        place = (
            lax.broadcasted_iota(jnp.int32, (chan_rows, total.shape[1]), 1)
            == 4 * lax.broadcasted_iota(jnp.int32, (chan_rows, total.shape[1]), 0) + q
        ).astype(BF16)
        total = total + jnp.dot(part, place, preferred_element_type=F32)
    out_ref[...] = total


def norm_kernel(tokens_ref, gain_ref, normed_ref, flipped_ref):
    wide = tokens_ref[...].astype(F32)
    mean = jnp.mean(wide, -1, keepdims=True)
    centred = wide - mean
    variance = jnp.mean(centred * centred, -1, keepdims=True)
    normed = (centred * lax.rsqrt(variance + EPS) * gain_ref[...]).astype(BF16)
    normed_ref[...] = normed
    flipped_ref[...] = normed.T


def norm_piece(piece, gain_row):
    features = piece.shape[-1]
    return pl.pallas_call(
        norm_kernel,
        out_shape=(
            jax.ShapeDtypeStruct((128, features), BF16),
            jax.ShapeDtypeStruct((features, 128), BF16),
        ),
        in_specs=vmem(2),
        out_specs=tuple(vmem(2)),
        compiler_params=params(8),
        cost_estimate=cost(2000000000, 8000000),
        name="norm",
    )(piece.reshape(128, features), gain_row)


def slope(value):
    return value * lax.rsqrt(value * value + DELTA * DELTA)


def pairs_kernel(
    place_ref, quad_ref, other_ref, bias_ref, truth_ref, wt_ref, *refs
):
    pieces = refs[:8]
    full_ref, bias_out_ref, *dfield_refs = refs[8:18]
    normed_ref, field, sums = refs[18:]
    for k in range(8):
        normed_ref[pl.ds(128 * k, 128), :] = pieces[k][...]
    width = full_ref.shape[1]
    padded = field.shape[2]
    count = 16
    coef = (1.0 - (1.0 - ALPHA) / count) / (count * (count - 1))
    for core, ref in ((0, quad_ref), (1, other_ref)):
        for yh, step in [(yh, step) for yh in range(2) for step in range(4)]:
            block = (
                (place_ref[0] ^ yh) * 8 + (place_ref[1] ^ step) * 2 + (place_ref[2] ^ core)
            )
            full_ref[pl.ds(pl.multiple_of(block * 96, 96), 96), :] = ref[step, yh]

    def project(step, carry):
        row = pl.multiple_of(step * 256, 256)
        part = jnp.dot(
            normed_ref[pl.ds(row, 256), :], full_ref[...], preferred_element_type=F32
        ) + bias_ref[...]
        part = part.astype(BF16).astype(F32).reshape(4, 64, width)
        field[pl.ds(step * 4, 4), :, 0:width] = part
        return carry

    lax.fori_loop(0, 4, project, 0)
    sums[...] = jnp.zeros_like(sums)
    tiles = padded // 128

    def pairs(step, carry):
        row = pl.multiple_of((step // tiles) * 8, 8)
        lane = pl.multiple_of((step % tiles) * 128, 128)
        here = (pl.ds(row, 8), pl.ds(lane, 128))
        values = [field[m, here[0], here[1]] for m in range(count)]
        total = [None] * count
        for m in range(count):
            for k in range(m + 1, count):
                s = slope(values[m] - values[k])
                total[m] = s if total[m] is None else total[m] + s
                total[k] = -s if total[k] is None else total[k] - s
        true = truth_ref[here[0], here[1]]
        scale = wt_ref[0:1, pl.ds(lane, 128)]
        column = None
        for m in range(count):
            value = scale * (slope(values[m] - true) * (1.0 / count) - coef * total[m])
            value = value.astype(BF16).astype(F32)
            field[m, here[0], here[1]] = value
            column = value if column is None else column + value
        sums[:, pl.ds(lane, 128)] += column
        return carry

    lax.fori_loop(0, 8 * tiles, pairs, 0)
    bias_out_ref[...] = jnp.sum(sums[...], axis=0, keepdims=True)

    for k in range(8):
        for m in range(2):
            dfield_refs[k][64 * m : 64 * m + 64, :] = field[2 * k + m, :, 0:width].astype(BF16)


def grad_kernel(place_ref, full_ref, bias_part_ref, gain_ref, *refs):
    pieces, fields = refs[:8], refs[8:16]
    keep_ref, send_ref, small_ref, flipped_ref, dfield_ref, grad, rows = refs[16:]
    for k in range(8):
        flipped_ref[:, pl.ds(128 * k, 128)] = pieces[k][...]
        dfield_ref[pl.ds(128 * k, 128), :] = fields[k][...]
    width = full_ref.shape[1]
    features = full_ref.shape[0]

    def weight_grad(step, carry):
        row = pl.multiple_of(step * 512, 512)
        grad[pl.ds(row, 512), :] = jnp.dot(
            flipped_ref[pl.ds(row, 512), :], dfield_ref[...], preferred_element_type=F32
        )
        return carry

    lax.fori_loop(0, features // 512, weight_grad, 0)

    def gain_part(step, carry):
        row = pl.multiple_of(step * 128, 128)
        part = jnp.sum(
            grad[pl.ds(row, 128), :] * full_ref[pl.ds(row, 128), :].astype(F32),
            axis=1, keepdims=True,
        )
        rows[:, pl.ds(row, 128)] = jnp.broadcast_to(part, (128, 128)).T[0:8]
        return carry

    lax.fori_loop(0, features // 128, gain_part, 0)
    small_ref[...] = jnp.zeros_like(small_ref)
    for n in range(3):
        cut = slice(512 * n, 512 * (n + 1))
        small_ref[n : n + 1, :] = rows[0:1, cut] / gain_ref[:, cut]
        stop = min(512 * (n + 1), width)
        small_ref[3 + n : 4 + n, 0 : stop - 512 * n] = bias_part_ref[:, 512 * n : stop]
    put_small(send_ref, small_ref[...])
    for yh in range(2):
        for step in range(4):
            base = (place_ref[0] ^ yh) * 8 + (place_ref[1] ^ step) * 2
            mine = pl.multiple_of((base + place_ref[2]) * 96, 96)
            other = pl.multiple_of((base + (place_ref[2] ^ 1)) * 96, 96)
            keep_ref[yh, step] = grad[pl.ds(mine, 96), :]
            start = 16 + 96 * (yh * 4 + step)
            send_ref[start : start + 96, :] = grad[pl.ds(other, 96), :].astype(BF16)


def backward_kernel(order, before, place_ref, tokens_ref, gain_ref, full_ref, *refs):
    count = len(order)
    earlier, pieces = refs[: len(before)], refs[len(before) : len(before) + count]
    out_ref, dfield, grad = refs[len(before) + count :]
    features = full_ref.shape[0]
    for n in range(count):
        dfield[pl.ds(128 * n, 128), :] = pieces[n][...]

    def matmul(step, carry):
        lane = pl.multiple_of(step * 256, 256)
        grad[:, pl.ds(lane, 256)] = lax.dot_general(
            dfield[...], full_ref[pl.ds(lane, 256), :], (((1,), (1,)), ((), ())),
            preferred_element_type=F32,
        )
        return carry

    lax.fori_loop(0, features // 256, matmul, 0)
    for n, k in enumerate(order):
        j = place_ref[3] ^ k

        def rows(m, carry, n=n, j=j):
            wide = tokens_ref[m, j].astype(F32)
            mean = jnp.mean(wide, -1, keepdims=True)
            centred = wide - mean
            variance = jnp.mean(centred * centred, -1, keepdims=True)
            inverse = lax.rsqrt(variance + EPS)
            xhat = centred * inverse
            start = pl.multiple_of(128 * n + m * 64, 64)
            scaled = grad[pl.ds(start, 64), :] * gain_ref[...]
            out = inverse * (
                scaled
                - jnp.mean(scaled, -1, keepdims=True)
                - xhat * jnp.mean(scaled * xhat, -1, keepdims=True)
            )
            if before:
                out_ref[m, j] = out.astype(BF16)
            else:
                out_ref[n, m] = out.astype(BF16)
            return carry

        lax.fori_loop(0, 2, rows, 0)
    for done, ref in zip(before, earlier):
        for n, k in enumerate(done):
            for m in range(2):
                out_ref[m, place_ref[3] ^ k] = ref[n, m]


def member_rows(parts, where):
    _, _, rows, width = parts.shape
    members = 8 * rows
    index = jnp.arange(members)
    block, inside = index // rows, index % rows
    source = (((block // 2) ^ where["x"]) * 2 + ((block % 2) ^ where["yl"])) * rows + inside
    pick = (source[:, None] == jnp.arange(members)[None, :]).astype(BF16)
    return jnp.dot(
        pick, parts.reshape(members, width), preferred_element_type=F32
    ).astype(BF16)


def put_small(ref, small):
    high = small.astype(BF16)
    low = (small - high.astype(F32)).astype(BF16)
    ref[0:16, :] = jnp.zeros((16, ref.shape[1]), BF16)
    ref[0:16, 0:512] = jnp.concatenate([high, low], axis=0)


def get_small(ref):
    rows = ref[0:16, 0:512].astype(F32)
    return rows[0:8] + rows[8:16]


def core_kernel(keep_ref, small_ref, came_ref, own_ref, small_out_ref, *sends):
    small = small_ref[...] + get_small(came_ref)
    small_out_ref[...] = small
    for step in range(4):
        for yh in range(2):
            start = 16 + 96 * (yh * 4 + step)
            block = keep_ref[yh, step] + came_ref[start : start + 96, :].astype(F32)
            if step == 0:
                own_ref[96 * yh : 96 * yh + 96, :] = block
            else:
                sends[step - 1][16 + 96 * yh : 112 + 96 * yh, :] = block.astype(BF16)
    for ref in sends:
        put_small(ref, small)


def iota(shape, axis):
    return lax.broadcasted_iota(jnp.int32, shape, axis)


def gather_sums(own_ref, small_ref, came):
    total, small = own_ref[...], small_ref[...]
    for ref in came:
        total = total + ref[16 : 16 + own_ref.shape[0], :].astype(F32)
        small = small + get_small(ref)
    return total, small


def z_kernel(own_ref, small_ref, a_ref, b_ref, c_ref, own_out_ref, small_out_ref, send_ref):
    total, small = gather_sums(own_ref, small_ref, (a_ref, b_ref, c_ref))
    small_out_ref[...] = small
    own_out_ref[...] = total[0:96]
    send_ref[16:112, :] = total[96:192].astype(BF16)
    put_small(send_ref, small)


def yh_kernel(own_ref, small_ref, came_ref, out_ref):
    total, small = gather_sums(own_ref, small_ref, (came_ref,))
    row, source = iota((128, 96), 0), iota((128, 96), 1)
    pick = (source == row // 16 * 12 + row % 16) & (row % 16 < 12)
    picked = jnp.dot(
        pick.astype(BF16), total.astype(BF16), preferred_element_type=F32
    ).astype(BF16)
    for n in range(8):
        put_small(out_ref.at[n], small)
        out_ref[n, 16:32, :] = picked[16 * n : 16 * n + 16]


def member_kernel(came_ref, share_ref, small_ref):
    total = came_ref[0, 16:32, :].astype(F32)
    small = get_small(came_ref.at[0])
    for n in range(1, 8):
        total = total + came_ref[n, 16:32, :].astype(F32)
        small = small + get_small(came_ref.at[n])
    share_ref[...] = total[0:12]
    for n in range(24):
        small_ref[n : n + 1, :] = small[n // 4 : n // 4 + 1, 128 * (n % 4) : 128 * (n % 4 + 1)]


def on_device(tokens, gain, weight, bias, target, channel_weight):
    where = {axis: lax.axis_index(axis) for axis in SIZE}
    member = where["x"] * 2 + where["yl"]
    space = (where["yh"] * 4 + where["z"]) * 2 + where["core"]
    place = jnp.stack(
        [where["yh"], where["z"], where["core"], member, where["x"], where["yl"]]
    ).astype(jnp.int32)
    smem = pl.BlockSpec(memory_space=pltpu.SMEM)
    features = tokens.shape[-1]
    outs = weight.shape[1]
    padded = -(-outs // 128) * 128
    gain_row = gain.reshape(1, features)

    pieces = tokens.reshape(2, 8, 64, features)
    sources = [
        lax.dynamic_index_in_dim(pieces, member ^ k, 1, keepdims=False) for k in range(8)
    ]
    t_here, l_here = member // 4, member % 4
    image = lax.dynamic_slice(
        target, (0, 4 * t_here, 256 * l_here), (target.shape[0], 4, 256)
    ).reshape(-1, 256)
    truth = pl.pallas_call(
        truth_kernel,
        out_shape=jax.ShapeDtypeStruct((64, padded), F32),
        in_specs=vmem(1),
        out_specs=vmem(1)[0],
        compiler_params=params(8),
        cost_estimate=cost(2000000000, 8000000),
        name="truth",
    )(image)
    table = jnp.asarray(latitude_weights(128).reshape(32, 4))
    latw = lax.dynamic_index_in_dim(table, space * 2 + t_here, 0, keepdims=False)
    wt = jnp.broadcast_to(
        channel_weight[:, None, None] * latw[None, :, None], (channel_weight.shape[0], 4, 4)
    ).reshape(1, outs)
    wt = jnp.pad(wt, ((0, 0), (0, padded - outs)))

    arrived = {0: sources[0], 4: swap_member(sources[4], 4)}
    near = jnp.stack([weight] + [swap_y(weight, k) for k in (1, 2, 3)])
    (p1,), (near,) = after((sources[1],), near)
    arrived[1] = swap_member(p1, 1)
    wide = jnp.stack([near] + [swap(near, "x", k) for k in (1, 2, 3)])
    (wide, p3, p6), (arrived[4], truth, wt) = after(
        (wide, sources[3], sources[6]), arrived[4], truth, wt
    )
    pair = jnp.stack([member_rows(wide[:, 2 * k : 2 * k + 2], where) for k in range(2)])
    quad = jnp.stack([pair] + [swap(pair, "z", k) for k in (1, 2, 3)])
    arrived[3], arrived[6] = swap_member(p3, 3), swap_member(p6, 6)
    (p7, p2), (arrived[1], arrived[6]) = after(
        (sources[7], sources[2]), arrived[1], arrived[6]
    )
    arrived[7], arrived[2] = swap_member(p7, 7), swap_member(p2, 2)
    (p5,), (arrived[3],) = after((sources[5],), arrived[3])
    arrived[5] = swap_member(p5, 5)
    early = (0, 4, 1, 3, 6)
    normed = {k: norm_piece(arrived[k], gain_row) for k in early}
    held = [n for k in early for n in normed[k]]
    (quad,), done = after((quad,), arrived[7], arrived[2], arrived[5], *held)
    arrived[7], arrived[2], arrived[5] = done[:3]
    for n, k in enumerate(early):
        normed[k] = done[3 + 2 * n : 5 + 2 * n]
    other = swap(quad, "core", 1)
    for k in (7, 2, 5):
        normed[k] = norm_piece(arrived[k], gain_row)

    full, bias_part, *dfield = pl.pallas_call(
        pairs_kernel,
        out_shape=(
            jax.ShapeDtypeStruct((features, outs), BF16),
            jax.ShapeDtypeStruct((1, padded), F32),
        )
        + (jax.ShapeDtypeStruct((128, outs), BF16),) * 8,
        in_specs=[smem] + vmem(13),
        out_specs=tuple(vmem(10)),
        scratch_shapes=[
            pltpu.VMEM((1024, features), BF16),
            pltpu.VMEM((16, 64, padded), F32),
            pltpu.VMEM((8, padded), F32),
        ],
        compiler_params=params(32),
        cost_estimate=cost(20000000000, 80000000),
        name="pairs",
    )(place, quad, other, bias.reshape(1, outs), truth, wt, *[normed[k][0] for k in range(8)])

    returned = {0: dfield[0]}
    for k in (1, 4):
        returned[k] = swap_member(dfield[k], k)
    keep, send, small = pl.pallas_call(
        grad_kernel,
        out_shape=(
            jax.ShapeDtypeStruct((2, 4, 96, outs), F32),
            jax.ShapeDtypeStruct((16 + 768, outs), BF16),
            jax.ShapeDtypeStruct((8, 512), F32),
        ),
        in_specs=[smem] + vmem(19),
        out_specs=tuple(vmem(3)),
        scratch_shapes=[
            pltpu.VMEM((features, 1024), BF16),
            pltpu.VMEM((1024, outs), BF16),
            pltpu.VMEM((features, outs), F32),
            pltpu.VMEM((8, features), F32),
        ],
        compiler_params=params(34),
        cost_estimate=cost(12000000000, 45000000),
        name="weight_gradient",
    )(
        place, full, bias_part, gain_row,
        *[normed[k][1] for k in range(8)], *dfield,
    )

    def backward(order, *before):
        count = len(order)
        shape = (2, 8, 64, features) if before else (count, 2, 64, features)
        return pl.pallas_call(
            functools.partial(backward_kernel, order, [done for done, _ in before]),
            out_shape=jax.ShapeDtypeStruct(shape, BF16),
            in_specs=[smem] + vmem(3 + count + len(before)),
            out_specs=vmem(1)[0],
            scratch_shapes=[
                pltpu.VMEM((128 * count, outs), BF16),
                pltpu.VMEM((128 * count, features), F32),
            ],
            compiler_params=params(32),
            cost_estimate=cost(1000, 1000),
            name="backward",
        )(
            place, pieces, gain_row, full,
            *[part for _, part in before], *[returned[k] for k in order],
        )

    def combine(kernel, name, own_rows, send_rows, sends, *operands):
        return pl.pallas_call(
            kernel,
            out_shape=(
                jax.ShapeDtypeStruct((own_rows, outs), F32),
                jax.ShapeDtypeStruct((8, 512), F32),
            )
            + (jax.ShapeDtypeStruct((send_rows, outs), BF16),) * sends,
            in_specs=([smem] if operands[0] is place else [])
            + vmem(len(operands) - (operands[0] is place)),
            out_specs=tuple(vmem(2 + sends)),
            compiler_params=params(16),
            cost_estimate=cost(1000000000, 4000000),
            name=name,
        )(*operands)

    (send,), done = after((send,), *[returned[k] for k in (1, 4)])
    for k, piece in zip((1, 4), done):
        returned[k] = piece
    came = swap(send, "core", 1)
    own, small, *sends = combine(core_kernel, "core_sums", 192, 208, 3, keep, small, came)
    came = [swap(value, "z", k) for k, value in zip((1, 2, 3), sends)]
    (d3, d6), (small,) = after((dfield[3], dfield[6]), small)
    returned[3], returned[6] = swap_member(d3, 3), swap_member(d6, 6)
    late = (7, 2, 5)
    held, (returned[3], returned[6]) = after(
        [dfield[k] for k in late], returned[3], returned[6]
    )
    for k, piece in zip(late, held):
        returned[k] = swap_member(piece, k)
    first = backward(FIRST)
    came, (first,) = after(came, first)
    own, small, send = combine(z_kernel, "z_sums", 96, 112, 1, own, small, *came)
    came = swap(send, "yh", 1)
    result = backward(SECOND, (FIRST, first))
    (came,), (result,) = after((came,), result)
    send = pl.pallas_call(
        yh_kernel,
        out_shape=jax.ShapeDtypeStruct((8, 32, outs), BF16),
        in_specs=vmem(3),
        out_specs=vmem(1)[0],
        compiler_params=params(16),
        cost_estimate=cost(1000000000, 4000000),
        name="yh_sums",
    )(own, small, came)
    came = lax.all_to_all(send, MEMBER, 0, 0)
    share, small = pl.pallas_call(
        member_kernel,
        out_shape=(
            jax.ShapeDtypeStruct((12, outs), F32),
            jax.ShapeDtypeStruct((24, 128), F32),
        ),
        in_specs=vmem(1),
        out_specs=tuple(vmem(2)),
        compiler_params=params(16),
        cost_estimate=cost(1000000000, 4000000),
        name="member_sums",
    )(came)
    small = small.reshape(-1)
    return (
        result.reshape(tokens.shape),
        small[:features],
        share,
        small[features : features + outs],
    )


def solution(mesh):
    fine = Mesh(
        mesh.devices.reshape(2, 4, 2, 4, 2), ("yh", "z", "core", "x", "yl")
    )
    both = SPACE + MEMBER
    return jax.shard_map(
        on_device,
        mesh=fine,
        in_specs=(
            P(MEMBER, SPACE, None, None),
            P(),
            P(both, None),
            P(),
            P(None, SPACE, None),
            P(),
        ),
        out_specs=(P(MEMBER, SPACE, None, None), P(), P(both, None), P()),
        check_vma=False,
    )
```

```python
import functools

import jax
import jax.numpy as jnp
import numpy as np
from jax import lax
from jax.experimental import pallas as pl
from jax.experimental.pallas import tpu as pltpu
from jax.sharding import Mesh
from jax.sharding import PartitionSpec as P

ALPHA = 0.95
DELTA = 0.1
EPS = 1e-05
SIZE = dict(yh=2, z=4, core=2, x=4, yl=2)
SPACE = ("yh", "z", "core")
MEMBER = ("x", "yl")
BF16 = jnp.bfloat16
FIRST, SECOND = (0, 1, 4), (3, 6, 7, 2, 5)
F32 = jnp.float32


def params(mebibytes):
    return pltpu.CompilerParams(vmem_limit_bytes=mebibytes * 1024 * 1024)


def cost(flops, bytes_accessed):
    return pl.CostEstimate(flops=flops, bytes_accessed=bytes_accessed, transcendentals=0)


def after(values, *done):
    out = lax.optimization_barrier((*values, *done))
    return out[: len(values)], out[len(values) :]


def latitude_weights(rows):
    index = np.arange(rows, dtype=np.float64)
    cosine = np.cos((60.0 - 0.25 * (index + 0.5)) * (np.pi / 180.0))
    return (cosine / cosine.mean()).astype(np.float32)


def swap(value, axis, step):
    return lax.ppermute(value, axis, [(i, i ^ step) for i in range(SIZE[axis])])


def swap_y(value, step):
    return lax.ppermute(value, ("yh", "yl"), [(i, i ^ step) for i in range(4)])


def swap_member(value, step):
    return lax.ppermute(value, MEMBER, [(i, i ^ step) for i in range(8)])


def vmem(count):
    return [pl.BlockSpec(memory_space=pltpu.VMEM)] * count


def truth_kernel(image_ref, out_ref):
    image = image_ref[...]
    chan_rows, cols = image.shape
    cells = cols // 4
    total = jnp.zeros(out_ref.shape, F32)
    for q in range(4):
        pick = (
            lax.broadcasted_iota(jnp.int32, (cells, cols), 1)
            == 4 * lax.broadcasted_iota(jnp.int32, (cells, cols), 0) + q
        ).astype(BF16)
        part = lax.dot_general(
            pick, image, (((1,), (1,)), ((), ())), preferred_element_type=F32
        ).astype(BF16)
        place = (
            lax.broadcasted_iota(jnp.int32, (chan_rows, total.shape[1]), 1)
            == 4 * lax.broadcasted_iota(jnp.int32, (chan_rows, total.shape[1]), 0) + q
        ).astype(BF16)
        total = total + jnp.dot(part, place, preferred_element_type=F32)
    out_ref[...] = total


def norm_kernel(tokens_ref, gain_ref, normed_ref, flipped_ref):
    wide = tokens_ref[...].astype(F32)
    mean = jnp.mean(wide, -1, keepdims=True)
    centred = wide - mean
    variance = jnp.mean(centred * centred, -1, keepdims=True)
    normed = (centred * lax.rsqrt(variance + EPS) * gain_ref[...]).astype(BF16)
    normed_ref[...] = normed
    flipped_ref[...] = normed.T


def norm_piece(piece, gain_row):
    features = piece.shape[-1]
    return pl.pallas_call(
        norm_kernel,
        out_shape=(
            jax.ShapeDtypeStruct((128, features), BF16),
            jax.ShapeDtypeStruct((features, 128), BF16),
        ),
        in_specs=vmem(2),
        out_specs=tuple(vmem(2)),
        compiler_params=params(8),
        cost_estimate=cost(2000000000, 8000000),
        name="norm",
    )(piece.reshape(128, features), gain_row)


def slope(value):
    return value * lax.rsqrt(value * value + DELTA * DELTA)


def fair_slopes(field, row, lane, true, scale, sums):
    count = 16
    coef = (1.0 - (1.0 - ALPHA) / count) / (count * (count - 1))
    here = (pl.ds(row, 8), pl.ds(lane, 128))
    values = [field[m, here[0], here[1]] for m in range(count)]
    total = [None] * count
    for m in range(count):
        for k in range(m + 1, count):
            s = slope(values[m] - values[k])
            total[m] = s if total[m] is None else total[m] + s
            total[k] = -s if total[k] is None else total[k] - s
    column = None
    for m in range(count):
        value = scale * (slope(values[m] - true) * (1.0 / count) - coef * total[m])
        value = value.astype(BF16).astype(F32)
        field[m, here[0], here[1]] = value
        column = value if column is None else column + value
    sums[:, pl.ds(lane, 128)] += column


def middle_kernel(place_ref, quad_ref, other_ref, bias_ref, truth_ref, wt_ref, gain_ref, *refs):
    pieces, turned = refs[:8], refs[8:16]
    full_ref, keep_ref, send_ref, small_ref = refs[16:20]
    dfield_refs = refs[20:28]
    normed, flipped, field0, field1, slopes0, slopes1, part, sums, rows = refs[28:]
    fields, slopes = (field0, field1), (slopes0, slopes1)
    features, width = full_ref.shape
    count = 16
    tiles = [(at, min(256, width - at)) for at in range(0, width, 256)]
    core = place_ref[2]
    for k in range(8):
        normed[pl.ds(128 * k, 128), :] = pieces[k][...]
        flipped[:, pl.ds(128 * k, 128)] = turned[k][...]
    for c, ref in ((0, quad_ref), (1, other_ref)):
        for yh, step in [(yh, step) for yh in range(2) for step in range(4)]:
            block = (place_ref[0] ^ yh) * 8 + (place_ref[1] ^ step) * 2 + (core ^ c)
            full_ref[pl.ds(pl.multiple_of(block * 96, 96), 96), :] = ref[step, yh]
    rows[...] = jnp.zeros_like(rows)
    sums[...] = jnp.zeros_like(sums)
    send_ref[0:16, :] = jnp.zeros((16, width), BF16)

    def project(tile, step):
        at, wide = tiles[tile]
        row = pl.multiple_of(step * 1024, 256)
        out = jnp.dot(
            normed[pl.ds(row, 1024), :], full_ref[:, at : at + wide],
            preferred_element_type=F32,
        ) + bias_ref[:, at : at + wide]
        out = out.astype(BF16).astype(F32).reshape(16, 64, wide)
        fields[tile % 2][pl.ds(step * 16, 16), :, 0:wide] = out

    def pairs(tile, step):
        at, wide = tiles[tile]
        field, out = fields[tile % 2], slopes[tile % 2]
        row = pl.multiple_of(step * 64, 16)
        for lane in range(0, wide, 128):
            scale = wt_ref[0:1, at + lane : at + lane + 128]
            for half in range(0, 64, 8):
                start = pl.multiple_of(row + half, 8)
                true = truth_ref[pl.ds(start, 8), at + lane : at + lane + 128]
                fair_slopes(field, start, lane, true, scale, sums.at[:, at : at + 256])
            for m in range(count):
                out[pl.ds(pl.multiple_of(64 * m + row, 16), 64), lane : lane + 128] = field[
                    m, pl.ds(row, 64), lane : lane + 128
                ].astype(BF16)

    def weight_grad(tile, step):
        at, wide = tiles[tile]
        row = pl.multiple_of(step * 1536, 384)
        out = jnp.dot(
            flipped[pl.ds(row, 1536), :], slopes[tile % 2][:, 0:wide],
            preferred_element_type=F32,
        )
        part[:, 0:wide] = out
        here = out * full_ref[pl.ds(row, 1536), at : at + wide].astype(F32)
        for lane in range(0, wide, 128):
            stop = min(lane + 128, wide)
            rows[pl.ds(row, 1536), 0 : stop - lane] += here[:, lane:stop]
        for q in range(8):
            mine = part[pl.ds(pl.multiple_of(192 * q + core * 96, 96), 96), 0:wide]
            other = part[pl.ds(pl.multiple_of(192 * q + (core ^ 1) * 96, 96), 96), 0:wide]
            keep_ref[8 * step + q, :, at : at + wide] = mine
            start = pl.multiple_of(16 + 96 * (8 * step + q), 16)
            send_ref[pl.ds(start, 96), at : at + wide] = other.astype(BF16)

    for phase in range(len(tiles) + 2):

        def body(step, carry, phase=phase):
            if phase - 2 >= 0:
                weight_grad(phase - 2, step)
            if phase < len(tiles):
                project(phase, step)
            if 0 <= phase - 1 < len(tiles):
                pairs(phase - 1, step)
            return carry

        lax.fori_loop(0, 1, body, 0)
        if 0 <= phase - 1 < len(tiles):
            at, wide = tiles[phase - 1]
            for k in range(8):
                dfield_refs[k][:, at : at + wide] = slopes[(phase - 1) % 2][
                    128 * k : 128 * k + 128, 0:wide
                ]
    small_ref[...] = jnp.zeros_like(small_ref)
    bias_sums = jnp.sum(sums[...], axis=0, keepdims=True)
    for n in range(3):
        turned_rows = jnp.concatenate(
            [rows[512 * n + 128 * q : 512 * n + 128 * q + 128, :].T for q in range(4)], axis=1
        )
        gain_sums = jnp.sum(turned_rows, axis=0, keepdims=True)
        small_ref[n : n + 1, :] = gain_sums / gain_ref[:, 512 * n : 512 * n + 512]
        stop = min(512 * (n + 1), width)
        small_ref[3 + n : 4 + n, 0 : stop - 512 * n] = bias_sums[:, 512 * n : stop]
    put_small(send_ref, small_ref[...])


def backward_kernel(order, before, place_ref, tokens_ref, gain_ref, full_ref, *refs):
    count = len(order)
    earlier, pieces = refs[: len(before)], refs[len(before) : len(before) + count]
    out_ref, dfield, grad = refs[len(before) + count :]
    features = full_ref.shape[0]
    for n in range(count):
        dfield[pl.ds(128 * n, 128), :] = pieces[n][...]

    def matmul(step, carry):
        lane = pl.multiple_of(step * 256, 256)
        grad[:, pl.ds(lane, 256)] = lax.dot_general(
            dfield[...], full_ref[pl.ds(lane, 256), :], (((1,), (1,)), ((), ())),
            preferred_element_type=F32,
        )
        return carry

    lax.fori_loop(0, features // 256, matmul, 0)
    for n, k in enumerate(order):
        j = place_ref[3] ^ k

        def rows(m, carry, n=n, j=j):
            wide = tokens_ref[m, j].astype(F32)
            mean = jnp.mean(wide, -1, keepdims=True)
            centred = wide - mean
            variance = jnp.mean(centred * centred, -1, keepdims=True)
            inverse = lax.rsqrt(variance + EPS)
            xhat = centred * inverse
            start = pl.multiple_of(128 * n + m * 64, 64)
            scaled = grad[pl.ds(start, 64), :] * gain_ref[...]
            out = inverse * (
                scaled
                - jnp.mean(scaled, -1, keepdims=True)
                - xhat * jnp.mean(scaled * xhat, -1, keepdims=True)
            )
            if before:
                out_ref[m, j] = out.astype(BF16)
            else:
                out_ref[n, m] = out.astype(BF16)
            return carry

        lax.fori_loop(0, 2, rows, 0)
    for done, ref in zip(before, earlier):
        for n, k in enumerate(done):
            for m in range(2):
                out_ref[m, place_ref[3] ^ k] = ref[n, m]


def member_rows(parts, where):
    _, _, rows, width = parts.shape
    members = 8 * rows
    index = jnp.arange(members)
    block, inside = index // rows, index % rows
    source = (((block // 2) ^ where["x"]) * 2 + ((block % 2) ^ where["yl"])) * rows + inside
    pick = (source[:, None] == jnp.arange(members)[None, :]).astype(BF16)
    return jnp.dot(
        pick, parts.reshape(members, width), preferred_element_type=F32
    ).astype(BF16)


def put_small(ref, small):
    high = small.astype(BF16)
    low = (small - high.astype(F32)).astype(BF16)
    ref[0:16, :] = jnp.zeros((16, ref.shape[1]), BF16)
    ref[0:16, 0:512] = jnp.concatenate([high, low], axis=0)


def get_small(ref):
    rows = ref[0:16, 0:512].astype(F32)
    return rows[0:8] + rows[8:16]


def core_kernel(place_ref, keep_ref, small_ref, came_ref, own_ref, small_out_ref, *sends):
    small = small_ref[...] + get_small(came_ref)
    small_out_ref[...] = small
    for step in range(4):
        for yh in range(2):
            n = (place_ref[0] ^ yh) * 4 + (place_ref[1] ^ step)
            start = pl.multiple_of(16 + 96 * n, 16)
            block = keep_ref[n] + came_ref[pl.ds(start, 96), :].astype(F32)
            if step == 0:
                own_ref[96 * yh : 96 * yh + 96, :] = block
            else:
                sends[step - 1][16 + 96 * yh : 112 + 96 * yh, :] = block.astype(BF16)
    for ref in sends:
        put_small(ref, small)


def iota(shape, axis):
    return lax.broadcasted_iota(jnp.int32, shape, axis)


def gather_sums(own_ref, small_ref, came):
    total, small = own_ref[...], small_ref[...]
    for ref in came:
        total = total + ref[16 : 16 + own_ref.shape[0], :].astype(F32)
        small = small + get_small(ref)
    return total, small


def z_kernel(own_ref, small_ref, a_ref, b_ref, c_ref, own_out_ref, small_out_ref, send_ref):
    total, small = gather_sums(own_ref, small_ref, (a_ref, b_ref, c_ref))
    small_out_ref[...] = small
    own_out_ref[...] = total[0:96]
    send_ref[16:112, :] = total[96:192].astype(BF16)
    put_small(send_ref, small)


def yh_kernel(own_ref, small_ref, came_ref, out_ref):
    total, small = gather_sums(own_ref, small_ref, (came_ref,))
    row, source = iota((128, 96), 0), iota((128, 96), 1)
    pick = (source == row // 16 * 12 + row % 16) & (row % 16 < 12)
    picked = jnp.dot(
        pick.astype(BF16), total.astype(BF16), preferred_element_type=F32
    ).astype(BF16)
    for n in range(8):
        put_small(out_ref.at[n], small)
        out_ref[n, 16:32, :] = picked[16 * n : 16 * n + 16]


def member_kernel(came_ref, share_ref, small_ref):
    total = came_ref[0, 16:32, :].astype(F32)
    small = get_small(came_ref.at[0])
    for n in range(1, 8):
        total = total + came_ref[n, 16:32, :].astype(F32)
        small = small + get_small(came_ref.at[n])
    share_ref[...] = total[0:12]
    for n in range(24):
        small_ref[n : n + 1, :] = small[n // 4 : n // 4 + 1, 128 * (n % 4) : 128 * (n % 4 + 1)]


def middle(*operands):
    features, outs = 1536, operands[3].shape[1]
    padded = operands[4].shape[1]
    return pl.pallas_call(
        middle_kernel,
        out_shape=(
            jax.ShapeDtypeStruct((features, outs), BF16),
            jax.ShapeDtypeStruct((8, 96, outs), F32),
            jax.ShapeDtypeStruct((16 + 768, outs), BF16),
            jax.ShapeDtypeStruct((8, 512), F32),
        )
        + (jax.ShapeDtypeStruct((128, outs), BF16),) * 8,
        in_specs=[pl.BlockSpec(memory_space=pltpu.SMEM)] + vmem(len(operands) - 1),
        out_specs=tuple(vmem(12)),
        scratch_shapes=[
            pltpu.VMEM((1024, features), BF16),
            pltpu.VMEM((features, 1024), BF16),
            pltpu.VMEM((16, 64, 256), F32),
            pltpu.VMEM((16, 64, 256), F32),
            pltpu.VMEM((1024, 256), BF16),
            pltpu.VMEM((1024, 256), BF16),
            pltpu.VMEM((1536, 256), F32),
            pltpu.VMEM((8, padded + 128), F32),
            pltpu.VMEM((features, 128), F32),
        ],
        compiler_params=params(28),
        cost_estimate=cost(20000000000, 80000000),
        name="middle",
    )(*operands)


def on_device(tokens, gain, weight, bias, target, channel_weight):
    where = {axis: lax.axis_index(axis) for axis in SIZE}
    member = where["x"] * 2 + where["yl"]
    space = (where["yh"] * 4 + where["z"]) * 2 + where["core"]
    place = jnp.stack(
        [where["yh"], where["z"], where["core"], member, where["x"], where["yl"]]
    ).astype(jnp.int32)
    smem = pl.BlockSpec(memory_space=pltpu.SMEM)
    features = tokens.shape[-1]
    outs = weight.shape[1]
    padded = -(-outs // 128) * 128
    gain_row = gain.reshape(1, features)

    pieces = tokens.reshape(2, 8, 64, features)
    sources = [
        lax.dynamic_index_in_dim(pieces, member ^ k, 1, keepdims=False) for k in range(8)
    ]
    t_here, l_here = member // 4, member % 4
    image = lax.dynamic_slice(
        target, (0, 4 * t_here, 256 * l_here), (target.shape[0], 4, 256)
    ).reshape(-1, 256)
    truth = pl.pallas_call(
        truth_kernel,
        out_shape=jax.ShapeDtypeStruct((64, padded), F32),
        in_specs=vmem(1),
        out_specs=vmem(1)[0],
        compiler_params=params(8),
        cost_estimate=cost(2000000000, 8000000),
        name="truth",
    )(image)
    table = jnp.asarray(latitude_weights(128).reshape(32, 4))
    latw = lax.dynamic_index_in_dim(table, space * 2 + t_here, 0, keepdims=False)
    wt = jnp.broadcast_to(
        channel_weight[:, None, None] * latw[None, :, None], (channel_weight.shape[0], 4, 4)
    ).reshape(1, outs)
    wt = jnp.pad(wt, ((0, 0), (0, padded - outs)))

    arrived = {0: sources[0], 4: swap_member(sources[4], 4)}
    near = jnp.stack([weight] + [swap_y(weight, k) for k in (1, 2, 3)])
    (p1,), (near,) = after((sources[1],), near)
    arrived[1] = swap_member(p1, 1)
    wide = jnp.stack([near] + [swap(near, "x", k) for k in (1, 2, 3)])
    (wide, p3, p6), (arrived[4], truth, wt) = after(
        (wide, sources[3], sources[6]), arrived[4], truth, wt
    )
    pair = jnp.stack([member_rows(wide[:, 2 * k : 2 * k + 2], where) for k in range(2)])
    quad = jnp.stack([pair] + [swap(pair, "z", k) for k in (1, 2, 3)])
    arrived[3], arrived[6] = swap_member(p3, 3), swap_member(p6, 6)
    (p7, p2), (arrived[1], arrived[6]) = after(
        (sources[7], sources[2]), arrived[1], arrived[6]
    )
    arrived[7], arrived[2] = swap_member(p7, 7), swap_member(p2, 2)
    (p5,), (arrived[3],) = after((sources[5],), arrived[3])
    arrived[5] = swap_member(p5, 5)
    early = (0, 4, 1, 3, 6)
    normed = {k: norm_piece(arrived[k], gain_row) for k in early}
    held = [n for k in early for n in normed[k]]
    (quad,), done = after((quad,), arrived[7], arrived[2], arrived[5], *held)
    arrived[7], arrived[2], arrived[5] = done[:3]
    for n, k in enumerate(early):
        normed[k] = done[3 + 2 * n : 5 + 2 * n]
    other = swap(quad, "core", 1)
    for k in (7, 2, 5):
        normed[k] = norm_piece(arrived[k], gain_row)

    full, keep, send, small, *dfield = middle(
        place, quad, other, bias.reshape(1, outs), truth, wt, gain_row,
        *[normed[k][0] for k in range(8)], *[normed[k][1] for k in range(8)],
    )

    returned = {0: dfield[0]}
    for k in (1, 4):
        returned[k] = swap_member(dfield[k], k)

    def backward(order, *before):
        count = len(order)
        shape = (2, 8, 64, features) if before else (count, 2, 64, features)
        return pl.pallas_call(
            functools.partial(backward_kernel, order, [done for done, _ in before]),
            out_shape=jax.ShapeDtypeStruct(shape, BF16),
            in_specs=[smem] + vmem(3 + count + len(before)),
            out_specs=vmem(1)[0],
            scratch_shapes=[
                pltpu.VMEM((128 * count, outs), BF16),
                pltpu.VMEM((128 * count, features), F32),
            ],
            compiler_params=params(32),
            cost_estimate=cost(1000, 1000),
            name="backward",
        )(
            place, pieces, gain_row, full,
            *[part for _, part in before], *[returned[k] for k in order],
        )

    def combine(kernel, name, own_rows, send_rows, sends, *operands):
        return pl.pallas_call(
            kernel,
            out_shape=(
                jax.ShapeDtypeStruct((own_rows, outs), F32),
                jax.ShapeDtypeStruct((8, 512), F32),
            )
            + (jax.ShapeDtypeStruct((send_rows, outs), BF16),) * sends,
            in_specs=([smem] if operands[0] is place else [])
            + vmem(len(operands) - (operands[0] is place)),
            out_specs=tuple(vmem(2 + sends)),
            compiler_params=params(16),
            cost_estimate=cost(1000000000, 4000000),
            name=name,
        )(*operands)

    came = swap(send, "core", 1)
    own, small, *sends = combine(core_kernel, "core_sums", 192, 208, 3, place, keep, small, came)
    came = [swap(value, "z", k) for k, value in zip((1, 2, 3), sends)]
    (d3, d6), (small,) = after((dfield[3], dfield[6]), small)
    returned[3], returned[6] = swap_member(d3, 3), swap_member(d6, 6)
    late = (7, 2, 5)
    held, (returned[3], returned[6]) = after(
        [dfield[k] for k in late], returned[3], returned[6]
    )
    for k, piece in zip(late, held):
        returned[k] = swap_member(piece, k)
    first = backward(FIRST)
    came, (first,) = after(came, first)
    own, small, send = combine(z_kernel, "z_sums", 96, 112, 1, own, small, *came)
    came = swap(send, "yh", 1)
    result = backward(SECOND, (FIRST, first))
    (came,), (result,) = after((came,), result)
    send = pl.pallas_call(
        yh_kernel,
        out_shape=jax.ShapeDtypeStruct((8, 32, outs), BF16),
        in_specs=vmem(3),
        out_specs=vmem(1)[0],
        compiler_params=params(16),
        cost_estimate=cost(1000000000, 4000000),
        name="yh_sums",
    )(own, small, came)
    came = lax.all_to_all(send, MEMBER, 0, 0)
    share, small = pl.pallas_call(
        member_kernel,
        out_shape=(
            jax.ShapeDtypeStruct((12, outs), F32),
            jax.ShapeDtypeStruct((24, 128), F32),
        ),
        in_specs=vmem(1),
        out_specs=tuple(vmem(2)),
        compiler_params=params(16),
        cost_estimate=cost(1000000000, 4000000),
        name="member_sums",
    )(came)
    small = small.reshape(-1)
    return (
        result.reshape(tokens.shape),
        small[:features],
        share,
        small[features : features + outs],
    )


def solution(mesh):
    fine = Mesh(
        mesh.devices.reshape(2, 4, 2, 4, 2), ("yh", "z", "core", "x", "yl")
    )
    both = SPACE + MEMBER
    return jax.shard_map(
        on_device,
        mesh=fine,
        in_specs=(
            P(MEMBER, SPACE, None, None),
            P(),
            P(both, None),
            P(),
            P(None, SPACE, None),
            P(),
        ),
        out_specs=(P(MEMBER, SPACE, None, None), P(), P(both, None), P()),
        check_vma=False,
    )
```

```python
import functools

import jax
import jax.numpy as jnp
import numpy as np
from jax import lax
from jax.experimental import pallas as pl
from jax.experimental.pallas import tpu as pltpu
from jax.sharding import Mesh
from jax.sharding import PartitionSpec as P

ALPHA = 0.95
DELTA = 0.1
EPS = 1e-05
SIZE = dict(yh=2, z=4, core=2, x=4, yl=2)
SPACE = ("yh", "z", "core")
MEMBER = ("x", "yl")
BF16 = jnp.bfloat16
FIRST, SECOND, THIRD = (0, 1, 4), (3, 6), (7, 2, 5)
F32 = jnp.float32


def params(mebibytes):
    return pltpu.CompilerParams(vmem_limit_bytes=mebibytes * 1024 * 1024)


def cost(flops, bytes_accessed):
    return pl.CostEstimate(flops=flops, bytes_accessed=bytes_accessed, transcendentals=0)


def after(values, *done):
    out = lax.optimization_barrier((*values, *done))
    return out[: len(values)], out[len(values) :]


def latitude_weights(rows):
    index = np.arange(rows, dtype=np.float64)
    cosine = np.cos((60.0 - 0.25 * (index + 0.5)) * (np.pi / 180.0))
    return (cosine / cosine.mean()).astype(np.float32)


def swap(value, axis, step):
    return lax.ppermute(value, axis, [(i, i ^ step) for i in range(SIZE[axis])])


def swap_y(value, step):
    return lax.ppermute(value, ("yh", "yl"), [(i, i ^ step) for i in range(4)])


def swap_member(value, step):
    return lax.ppermute(value, MEMBER, [(i, i ^ step) for i in range(8)])


def vmem(count):
    return [pl.BlockSpec(memory_space=pltpu.VMEM)] * count


def truth_kernel(image_ref, out_ref):
    image = image_ref[...]
    chan_rows, cols = image.shape
    cells = cols // 4
    total = jnp.zeros(out_ref.shape, F32)
    for q in range(4):
        pick = (
            lax.broadcasted_iota(jnp.int32, (cells, cols), 1)
            == 4 * lax.broadcasted_iota(jnp.int32, (cells, cols), 0) + q
        ).astype(BF16)
        part = lax.dot_general(
            pick, image, (((1,), (1,)), ((), ())), preferred_element_type=F32
        ).astype(BF16)
        place = (
            lax.broadcasted_iota(jnp.int32, (chan_rows, total.shape[1]), 1)
            == 4 * lax.broadcasted_iota(jnp.int32, (chan_rows, total.shape[1]), 0) + q
        ).astype(BF16)
        total = total + jnp.dot(part, place, preferred_element_type=F32)
    out_ref[...] = total


def norm_kernel(tokens_ref, gain_ref, normed_ref, flipped_ref):
    wide = tokens_ref[...].astype(F32)
    mean = jnp.mean(wide, -1, keepdims=True)
    centred = wide - mean
    variance = jnp.mean(centred * centred, -1, keepdims=True)
    normed = (centred * lax.rsqrt(variance + EPS) * gain_ref[...]).astype(BF16)
    normed_ref[...] = normed
    flipped_ref[...] = normed.T


def norm_piece(piece, gain_row):
    features = piece.shape[-1]
    return pl.pallas_call(
        norm_kernel,
        out_shape=(
            jax.ShapeDtypeStruct((128, features), BF16),
            jax.ShapeDtypeStruct((features, 128), BF16),
        ),
        in_specs=vmem(2),
        out_specs=tuple(vmem(2)),
        compiler_params=params(8),
        cost_estimate=cost(2000000000, 8000000),
        name="norm",
    )(piece.reshape(128, features), gain_row)


def slope(value):
    return value * lax.rsqrt(value * value + DELTA * DELTA)


def fair_slopes(field, row, lane, true, scale, sums):
    count = 16
    coef = (1.0 - (1.0 - ALPHA) / count) / (count * (count - 1))
    here = (pl.ds(row, 8), pl.ds(lane, 128))
    values = [field[m, here[0], here[1]] for m in range(count)]
    total = [None] * count
    for m in range(count):
        for k in range(m + 1, count):
            s = slope(values[m] - values[k])
            total[m] = s if total[m] is None else total[m] + s
            total[k] = -s if total[k] is None else total[k] - s
    column = None
    for m in range(count):
        value = scale * (slope(values[m] - true) * (1.0 / count) - coef * total[m])
        value = value.astype(BF16).astype(F32)
        field[m, here[0], here[1]] = value
        column = value if column is None else column + value
    sums[:, pl.ds(lane, 128)] += column


def middle_kernel(place_ref, quad_ref, other_ref, bias_ref, truth_ref, wt_ref, gain_ref, *refs):
    pieces, turned = refs[:8], refs[8:16]
    full_ref, keep_ref, send_ref, small_ref = refs[16:20]
    dfield_refs = refs[20:28]
    normed, flipped, field0, field1, slopes0, slopes1, part, sums, rows = refs[28:]
    fields, slopes = (field0, field1), (slopes0, slopes1)
    features, width = full_ref.shape
    count = 16
    tiles = [(at, min(256, width - at)) for at in range(0, width, 256)]
    core = place_ref[2]
    for k in range(8):
        normed[pl.ds(128 * k, 128), :] = pieces[k][...]
        flipped[:, pl.ds(128 * k, 128)] = turned[k][...]
    for c, ref in ((0, quad_ref), (1, other_ref)):
        for yh, step in [(yh, step) for yh in range(2) for step in range(4)]:
            block = (place_ref[0] ^ yh) * 8 + (place_ref[1] ^ step) * 2 + (core ^ c)
            full_ref[pl.ds(pl.multiple_of(block * 96, 96), 96), :] = ref[step, yh]
    rows[...] = jnp.zeros_like(rows)
    sums[...] = jnp.zeros_like(sums)
    send_ref[0:16, :] = jnp.zeros((16, width), BF16)

    def project(tile, step):
        at, wide = tiles[tile]
        row = pl.multiple_of(step * 1024, 256)
        out = jnp.dot(
            normed[pl.ds(row, 1024), :], full_ref[:, at : at + wide],
            preferred_element_type=F32,
        ) + bias_ref[:, at : at + wide]
        out = out.astype(BF16).astype(F32).reshape(16, 64, wide)
        fields[tile % 2][pl.ds(step * 16, 16), :, 0:wide] = out

    def pairs(tile, step):
        at, wide = tiles[tile]
        field, out = fields[tile % 2], slopes[tile % 2]
        row = pl.multiple_of(step * 64, 16)
        for lane in range(0, wide, 128):
            scale = wt_ref[0:1, at + lane : at + lane + 128]
            for half in range(0, 64, 8):
                start = pl.multiple_of(row + half, 8)
                true = truth_ref[pl.ds(start, 8), at + lane : at + lane + 128]
                fair_slopes(field, start, lane, true, scale, sums.at[:, at : at + 256])
            for m in range(count):
                out[pl.ds(pl.multiple_of(64 * m + row, 16), 64), lane : lane + 128] = field[
                    m, pl.ds(row, 64), lane : lane + 128
                ].astype(BF16)

    def weight_grad(tile, step):
        at, wide = tiles[tile]
        row = pl.multiple_of(step * 1536, 384)
        out = jnp.dot(
            flipped[pl.ds(row, 1536), :], slopes[tile % 2][:, 0:wide],
            preferred_element_type=F32,
        )
        part[:, 0:wide] = out
        here = out * full_ref[pl.ds(row, 1536), at : at + wide].astype(F32)
        for lane in range(0, wide, 128):
            stop = min(lane + 128, wide)
            rows[pl.ds(row, 1536), 0 : stop - lane] += here[:, lane:stop]
        for q in range(8):
            mine = part[pl.ds(pl.multiple_of(192 * q + core * 96, 96), 96), 0:wide]
            other = part[pl.ds(pl.multiple_of(192 * q + (core ^ 1) * 96, 96), 96), 0:wide]
            keep_ref[8 * step + q, :, at : at + wide] = mine
            start = pl.multiple_of(16 + 96 * (8 * step + q), 16)
            send_ref[pl.ds(start, 96), at : at + wide] = other.astype(BF16)

    for phase in range(len(tiles) + 2):

        def body(step, carry, phase=phase):
            if phase - 2 >= 0:
                weight_grad(phase - 2, step)
            if phase < len(tiles):
                project(phase, step)
            if 0 <= phase - 1 < len(tiles):
                pairs(phase - 1, step)
            return carry

        lax.fori_loop(0, 1, body, 0)
        if 0 <= phase - 1 < len(tiles):
            at, wide = tiles[phase - 1]
            for k in range(8):
                dfield_refs[k][:, at : at + wide] = slopes[(phase - 1) % 2][
                    128 * k : 128 * k + 128, 0:wide
                ]
    small_ref[...] = jnp.zeros_like(small_ref)
    bias_sums = jnp.sum(sums[...], axis=0, keepdims=True)
    for n in range(3):
        turned_rows = jnp.concatenate(
            [rows[512 * n + 128 * q : 512 * n + 128 * q + 128, :].T for q in range(4)], axis=1
        )
        gain_sums = jnp.sum(turned_rows, axis=0, keepdims=True)
        small_ref[n : n + 1, :] = gain_sums / gain_ref[:, 512 * n : 512 * n + 512]
        stop = min(512 * (n + 1), width)
        small_ref[3 + n : 4 + n, 0 : stop - 512 * n] = bias_sums[:, 512 * n : stop]
    put_small(send_ref, small_ref[...])


def backward_kernel(order, before, place_ref, tokens_ref, gain_ref, full_ref, *refs):
    count = len(order)
    earlier, pieces = refs[: len(before)], refs[len(before) : len(before) + count]
    out_ref, dfield, grad = refs[len(before) + count :]
    features = full_ref.shape[0]
    for n in range(count):
        dfield[pl.ds(128 * n, 128), :] = pieces[n][...]

    def matmul(step, carry):
        lane = pl.multiple_of(step * 256, 256)
        grad[:, pl.ds(lane, 256)] = lax.dot_general(
            dfield[...], full_ref[pl.ds(lane, 256), :], (((1,), (1,)), ((), ())),
            preferred_element_type=F32,
        )
        return carry

    lax.fori_loop(0, features // 256, matmul, 0)
    for n, k in enumerate(order):
        j = place_ref[3] ^ k

        def rows(m, carry, n=n, j=j):
            wide = tokens_ref[m, j].astype(F32)
            mean = jnp.mean(wide, -1, keepdims=True)
            centred = wide - mean
            variance = jnp.mean(centred * centred, -1, keepdims=True)
            inverse = lax.rsqrt(variance + EPS)
            xhat = centred * inverse
            start = pl.multiple_of(128 * n + m * 64, 64)
            scaled = grad[pl.ds(start, 64), :] * gain_ref[...]
            out = inverse * (
                scaled
                - jnp.mean(scaled, -1, keepdims=True)
                - xhat * jnp.mean(scaled * xhat, -1, keepdims=True)
            )
            if before:
                out_ref[m, j] = out.astype(BF16)
            else:
                out_ref[n, m] = out.astype(BF16)
            return carry

        lax.fori_loop(0, 2, rows, 0)
    for done, ref in zip(before, earlier):
        for n, k in enumerate(done):
            for m in range(2):
                out_ref[m, place_ref[3] ^ k] = ref[n, m]


def member_rows(parts, where):
    _, _, rows, width = parts.shape
    members = 8 * rows
    index = jnp.arange(members)
    block, inside = index // rows, index % rows
    source = (((block // 2) ^ where["x"]) * 2 + ((block % 2) ^ where["yl"])) * rows + inside
    pick = (source[:, None] == jnp.arange(members)[None, :]).astype(BF16)
    return jnp.dot(
        pick, parts.reshape(members, width), preferred_element_type=F32
    ).astype(BF16)


def put_small(ref, small):
    high = small.astype(BF16)
    low = (small - high.astype(F32)).astype(BF16)
    ref[0:16, :] = jnp.zeros((16, ref.shape[1]), BF16)
    ref[0:16, 0:512] = jnp.concatenate([high, low], axis=0)


def get_small(ref):
    rows = ref[0:16, 0:512].astype(F32)
    return rows[0:8] + rows[8:16]


def core_kernel(place_ref, keep_ref, small_ref, came_ref, own_ref, small_out_ref, *sends):
    small = small_ref[...] + get_small(came_ref)
    small_out_ref[...] = small
    for step in range(4):
        for yh in range(2):
            n = (place_ref[0] ^ yh) * 4 + (place_ref[1] ^ step)
            start = pl.multiple_of(16 + 96 * n, 16)
            block = keep_ref[n] + came_ref[pl.ds(start, 96), :].astype(F32)
            if step == 0:
                own_ref[96 * yh : 96 * yh + 96, :] = block
            else:
                sends[step - 1][16 + 96 * yh : 112 + 96 * yh, :] = block.astype(BF16)
    for ref in sends:
        put_small(ref, small)


def iota(shape, axis):
    return lax.broadcasted_iota(jnp.int32, shape, axis)


def gather_sums(own_ref, small_ref, came):
    total, small = own_ref[...], small_ref[...]
    for ref in came:
        total = total + ref[16 : 16 + own_ref.shape[0], :].astype(F32)
        small = small + get_small(ref)
    return total, small


def z_kernel(own_ref, small_ref, a_ref, b_ref, c_ref, own_out_ref, small_out_ref, send_ref):
    total, small = gather_sums(own_ref, small_ref, (a_ref, b_ref, c_ref))
    small_out_ref[...] = small
    own_out_ref[...] = total[0:96]
    send_ref[16:112, :] = total[96:192].astype(BF16)
    put_small(send_ref, small)


def yh_kernel(own_ref, small_ref, came_ref, out_ref):
    total, small = gather_sums(own_ref, small_ref, (came_ref,))
    row, source = iota((128, 96), 0), iota((128, 96), 1)
    pick = (source == row // 16 * 12 + row % 16) & (row % 16 < 12)
    picked = jnp.dot(
        pick.astype(BF16), total.astype(BF16), preferred_element_type=F32
    ).astype(BF16)
    for n in range(8):
        put_small(out_ref.at[n], small)
        out_ref[n, 16:32, :] = picked[16 * n : 16 * n + 16]


def member_kernel(came_ref, share_ref, gain_out_ref, bias_out_ref):
    total = came_ref[0, 16:32, :].astype(F32)
    small = get_small(came_ref.at[0])
    for n in range(1, 8):
        total = total + came_ref[n, 16:32, :].astype(F32)
        small = small + get_small(came_ref.at[n])
    share_ref[...] = total[0:12]
    for n in range(21):
        ref, at = (gain_out_ref, n) if n < 12 else (bias_out_ref, n - 12)
        ref[at : at + 1, :] = small[n // 4 : n // 4 + 1, 128 * (n % 4) : 128 * (n % 4 + 1)]


def middle(*operands):
    features, outs = 1536, operands[3].shape[1]
    padded = operands[4].shape[1]
    return pl.pallas_call(
        middle_kernel,
        out_shape=(
            jax.ShapeDtypeStruct((features, outs), BF16),
            jax.ShapeDtypeStruct((8, 96, outs), F32),
            jax.ShapeDtypeStruct((16 + 768, outs), BF16),
            jax.ShapeDtypeStruct((8, 512), F32),
        )
        + (jax.ShapeDtypeStruct((128, outs), BF16),) * 8,
        in_specs=[pl.BlockSpec(memory_space=pltpu.SMEM)] + vmem(len(operands) - 1),
        out_specs=tuple(vmem(12)),
        scratch_shapes=[
            pltpu.VMEM((1024, features), BF16),
            pltpu.VMEM((features, 1024), BF16),
            pltpu.VMEM((16, 64, 256), F32),
            pltpu.VMEM((16, 64, 256), F32),
            pltpu.VMEM((1024, 256), BF16),
            pltpu.VMEM((1024, 256), BF16),
            pltpu.VMEM((1536, 256), F32),
            pltpu.VMEM((8, padded + 128), F32),
            pltpu.VMEM((features, 128), F32),
        ],
        compiler_params=params(28),
        cost_estimate=cost(20000000000, 80000000),
        name="middle",
    )(*operands)


def on_device(tokens, gain, weight, bias, target, channel_weight):
    where = {axis: lax.axis_index(axis) for axis in SIZE}
    member = where["x"] * 2 + where["yl"]
    space = (where["yh"] * 4 + where["z"]) * 2 + where["core"]
    place = jnp.stack(
        [where["yh"], where["z"], where["core"], member, where["x"], where["yl"]]
    ).astype(jnp.int32)
    smem = pl.BlockSpec(memory_space=pltpu.SMEM)
    features = tokens.shape[-1]
    outs = weight.shape[1]
    padded = -(-outs // 128) * 128
    gain_row = gain.reshape(1, features)

    pieces = tokens.reshape(2, 8, 64, features)
    sources = [
        lax.dynamic_index_in_dim(pieces, member ^ k, 1, keepdims=False) for k in range(8)
    ]
    t_here, l_here = member // 4, member % 4
    image = lax.dynamic_slice(
        target, (0, 4 * t_here, 256 * l_here), (target.shape[0], 4, 256)
    ).reshape(-1, 256)
    truth = pl.pallas_call(
        truth_kernel,
        out_shape=jax.ShapeDtypeStruct((64, padded), F32),
        in_specs=vmem(1),
        out_specs=vmem(1)[0],
        compiler_params=params(8),
        cost_estimate=cost(2000000000, 8000000),
        name="truth",
    )(image)
    table = jnp.asarray(latitude_weights(128).reshape(32, 4))
    latw = lax.dynamic_index_in_dim(table, space * 2 + t_here, 0, keepdims=False)
    wt = jnp.broadcast_to(
        channel_weight[:, None, None] * latw[None, :, None], (channel_weight.shape[0], 4, 4)
    ).reshape(1, outs)
    wt = jnp.pad(wt, ((0, 0), (0, padded - outs)))

    arrived = {0: sources[0], 4: swap_member(sources[4], 4)}
    near = jnp.stack([weight] + [swap_y(weight, k) for k in (1, 2, 3)])
    (p1,), (near,) = after((sources[1],), near)
    arrived[1] = swap_member(p1, 1)
    wide = jnp.stack([near] + [swap(near, "x", k) for k in (1, 2, 3)])
    (wide, p3, p6), (arrived[4], truth, wt) = after(
        (wide, sources[3], sources[6]), arrived[4], truth, wt
    )
    pair = jnp.stack([member_rows(wide[:, 2 * k : 2 * k + 2], where) for k in range(2)])
    quad = jnp.stack([pair] + [swap(pair, "z", k) for k in (1, 2, 3)])
    arrived[3], arrived[6] = swap_member(p3, 3), swap_member(p6, 6)
    (p7, p2), (arrived[1], arrived[6]) = after(
        (sources[7], sources[2]), arrived[1], arrived[6]
    )
    arrived[7], arrived[2] = swap_member(p7, 7), swap_member(p2, 2)
    (p5,), (arrived[3],) = after((sources[5],), arrived[3])
    arrived[5] = swap_member(p5, 5)
    early = (0, 4, 1, 3, 6)
    normed = {k: norm_piece(arrived[k], gain_row) for k in early}
    held = [n for k in early for n in normed[k]]
    (quad,), done = after((quad,), arrived[7], arrived[2], arrived[5], *held)
    arrived[7], arrived[2], arrived[5] = done[:3]
    for n, k in enumerate(early):
        normed[k] = done[3 + 2 * n : 5 + 2 * n]
    other = swap(quad, "core", 1)
    for k in (7, 2, 5):
        normed[k] = norm_piece(arrived[k], gain_row)

    full, keep, send, small, *dfield = middle(
        place, quad, other, bias.reshape(1, outs), truth, wt, gain_row,
        *[normed[k][0] for k in range(8)], *[normed[k][1] for k in range(8)],
    )

    returned = {0: dfield[0]}
    for k in (1, 4):
        returned[k] = swap_member(dfield[k], k)

    def backward(order, *before):
        count = len(order)
        shape = (2, 8, 64, features) if before else (count, 2, 64, features)
        return pl.pallas_call(
            functools.partial(backward_kernel, order, [done for done, _ in before]),
            out_shape=jax.ShapeDtypeStruct(shape, BF16),
            in_specs=[smem] + vmem(3 + count + len(before)),
            out_specs=vmem(1)[0],
            scratch_shapes=[
                pltpu.VMEM((128 * count, outs), BF16),
                pltpu.VMEM((128 * count, features), F32),
            ],
            compiler_params=params(32),
            cost_estimate=cost(1000, 1000),
            name="backward",
        )(
            place, pieces, gain_row, full,
            *[part for _, part in before], *[returned[k] for k in order],
        )

    def combine(kernel, name, own_rows, send_rows, sends, *operands):
        return pl.pallas_call(
            kernel,
            out_shape=(
                jax.ShapeDtypeStruct((own_rows, outs), F32),
                jax.ShapeDtypeStruct((8, 512), F32),
            )
            + (jax.ShapeDtypeStruct((send_rows, outs), BF16),) * sends,
            in_specs=([smem] if operands[0] is place else [])
            + vmem(len(operands) - (operands[0] is place)),
            out_specs=tuple(vmem(2 + sends)),
            compiler_params=params(16),
            cost_estimate=cost(1000000000, 4000000),
            name=name,
        )(*operands)

    came = swap(send, "core", 1)
    own, small, *sends = combine(core_kernel, "core_sums", 192, 208, 3, place, keep, small, came)
    came = [swap(value, "z", k) for k, value in zip((1, 2, 3), sends)]
    (d3, d6), (small,) = after((dfield[3], dfield[6]), small)
    returned[3], returned[6] = swap_member(d3, 3), swap_member(d6, 6)
    late = (7, 2, 5)
    held, (returned[3], returned[6]) = after(
        [dfield[k] for k in late], returned[3], returned[6]
    )
    for k, piece in zip(late, held):
        returned[k] = swap_member(piece, k)
    first, second = backward(FIRST), backward(SECOND)
    came, (first, second) = after(came, first, second)
    own, small, send = combine(z_kernel, "z_sums", 96, 112, 1, own, small, *came)
    came = swap(send, "yh", 1)
    result = backward(THIRD, (FIRST, first), (SECOND, second))
    (came,), (result,) = after((came,), result)
    send = pl.pallas_call(
        yh_kernel,
        out_shape=jax.ShapeDtypeStruct((8, 32, outs), BF16),
        in_specs=vmem(3),
        out_specs=vmem(1)[0],
        compiler_params=params(16),
        cost_estimate=cost(1000000000, 4000000),
        name="yh_sums",
    )(own, small, came)
    came = lax.all_to_all(send, MEMBER, 0, 0)
    share, gain_sums, bias_sums = pl.pallas_call(
        member_kernel,
        out_shape=(
            jax.ShapeDtypeStruct((12, outs), F32),
            jax.ShapeDtypeStruct((12, 128), F32),
            jax.ShapeDtypeStruct((9, 128), F32),
        ),
        in_specs=vmem(1),
        out_specs=tuple(vmem(3)),
        compiler_params=params(16),
        cost_estimate=cost(1000000000, 4000000),
        name="member_sums",
    )(came)
    return (
        result.reshape(tokens.shape),
        gain_sums.reshape(-1),
        share,
        bias_sums.reshape(-1)[:outs],
    )


def solution(mesh):
    fine = Mesh(
        mesh.devices.reshape(2, 4, 2, 4, 2), ("yh", "z", "core", "x", "yl")
    )
    both = SPACE + MEMBER
    return jax.shard_map(
        on_device,
        mesh=fine,
        in_specs=(
            P(MEMBER, SPACE, None, None),
            P(),
            P(both, None),
            P(),
            P(None, SPACE, None),
            P(),
        ),
        out_specs=(P(MEMBER, SPACE, None, None), P(), P(both, None), P()),
        check_vma=False,
    )
```

```python
import functools

import jax
import jax.numpy as jnp
import numpy as np
from jax import lax
from jax.experimental import pallas as pl
from jax.experimental.pallas import tpu as pltpu
from jax.sharding import Mesh
from jax.sharding import PartitionSpec as P

ALPHA = 0.95
DELTA = 0.1
EPS = 1e-05
SIZE = dict(yh=2, z=4, core=2, x=4, yl=2)
SPACE = ("yh", "z", "core")
MEMBER = ("x", "yl")
BF16 = jnp.bfloat16
FIRST, SECOND, THIRD = (0, 1, 4), (3, 6), (7, 2, 5)
F32 = jnp.float32


def params(mebibytes):
    return pltpu.CompilerParams(vmem_limit_bytes=mebibytes * 1024 * 1024)


def cost(flops, bytes_accessed):
    return pl.CostEstimate(flops=flops, bytes_accessed=bytes_accessed, transcendentals=0)


def after(values, *done):
    out = lax.optimization_barrier((*values, *done))
    return out[: len(values)], out[len(values) :]


def latitude_weights(rows):
    index = np.arange(rows, dtype=np.float64)
    cosine = np.cos((60.0 - 0.25 * (index + 0.5)) * (np.pi / 180.0))
    return (cosine / cosine.mean()).astype(np.float32)


def swap(value, axis, step):
    return lax.ppermute(value, axis, [(i, i ^ step) for i in range(SIZE[axis])])


def swap_y(value, step):
    return lax.ppermute(value, ("yh", "yl"), [(i, i ^ step) for i in range(4)])


def swap_member(value, step):
    return lax.ppermute(value, MEMBER, [(i, i ^ step) for i in range(8)])


def vmem(count):
    return [pl.BlockSpec(memory_space=pltpu.VMEM)] * count


def truth_kernel(image_ref, out_ref):
    image = image_ref[...]
    chan_rows, cols = image.shape
    cells = cols // 4
    total = jnp.zeros(out_ref.shape, F32)
    for q in range(4):
        pick = (
            lax.broadcasted_iota(jnp.int32, (cells, cols), 1)
            == 4 * lax.broadcasted_iota(jnp.int32, (cells, cols), 0) + q
        ).astype(BF16)
        part = lax.dot_general(
            pick, image, (((1,), (1,)), ((), ())), preferred_element_type=F32
        ).astype(BF16)
        place = (
            lax.broadcasted_iota(jnp.int32, (chan_rows, total.shape[1]), 1)
            == 4 * lax.broadcasted_iota(jnp.int32, (chan_rows, total.shape[1]), 0) + q
        ).astype(BF16)
        total = total + jnp.dot(part, place, preferred_element_type=F32)
    out_ref[...] = total


def norm_kernel(tokens_ref, gain_ref, normed_ref, flipped_ref):
    wide = tokens_ref[...].astype(F32)
    mean = jnp.mean(wide, -1, keepdims=True)
    centred = wide - mean
    variance = jnp.mean(centred * centred, -1, keepdims=True)
    normed = (centred * lax.rsqrt(variance + EPS) * gain_ref[...]).astype(BF16)
    normed_ref[...] = normed
    flipped_ref[...] = normed.T


def norm_piece(piece, gain_row):
    features = piece.shape[-1]
    return pl.pallas_call(
        norm_kernel,
        out_shape=(
            jax.ShapeDtypeStruct((128, features), BF16),
            jax.ShapeDtypeStruct((features, 128), BF16),
        ),
        in_specs=vmem(2),
        out_specs=tuple(vmem(2)),
        compiler_params=params(8),
        cost_estimate=cost(2000000000, 8000000),
        name="norm",
    )(piece.reshape(128, features), gain_row)


def slope(value):
    return value * lax.rsqrt(value * value + DELTA * DELTA)


def fair_slopes(field, row, lane, true, scale, sums):
    count = 16
    coef = (1.0 - (1.0 - ALPHA) / count) / (count * (count - 1))
    here = (pl.ds(row, 8), pl.ds(lane, 128))
    values = [field[m, here[0], here[1]] for m in range(count)]
    total = [None] * count
    for m in range(count):
        for k in range(m + 1, count):
            s = slope(values[m] - values[k])
            total[m] = s if total[m] is None else total[m] + s
            total[k] = -s if total[k] is None else total[k] - s
    column = None
    for m in range(count):
        value = scale * (slope(values[m] - true) * (1.0 / count) - coef * total[m])
        value = value.astype(BF16).astype(F32)
        field[m, here[0], here[1]] = value
        column = value if column is None else column + value
    sums[:, pl.ds(lane, 128)] += column


def middle_kernel(place_ref, quad_ref, other_ref, bias_ref, truth_ref, wt_ref, gain_ref, *refs):
    pieces, turned = refs[:8], refs[8:16]
    full_ref, keep_ref, send_ref, small_ref = refs[16:20]
    dfield_refs = refs[20:28]
    normed, flipped, field0, field1, slopes0, slopes1, part, sums, rows = refs[28:]
    fields, slopes = (field0, field1), (slopes0, slopes1)
    features, width = full_ref.shape
    count = 16
    tiles = [(at, min(256, width - at)) for at in range(0, width, 256)]
    core = place_ref[2]
    for k in range(8):
        normed[pl.ds(128 * k, 128), :] = pieces[k][...]
        flipped[:, pl.ds(128 * k, 128)] = turned[k][...]
    for c, ref in ((0, quad_ref), (1, other_ref)):
        for yh, step in [(yh, step) for yh in range(2) for step in range(4)]:
            block = (place_ref[0] ^ yh) * 8 + (place_ref[1] ^ step) * 2 + (core ^ c)
            full_ref[pl.ds(pl.multiple_of(block * 96, 96), 96), :] = ref[step, yh]
    rows[...] = jnp.zeros_like(rows)
    sums[...] = jnp.zeros_like(sums)
    send_ref[0:16, :] = jnp.zeros((16, width), BF16)

    def project(tile, step):
        at, wide = tiles[tile]
        row = pl.multiple_of(step * 1024, 256)
        out = jnp.dot(
            normed[pl.ds(row, 1024), :], full_ref[:, at : at + wide],
            preferred_element_type=F32,
        ) + bias_ref[:, at : at + wide]
        out = out.astype(BF16).astype(F32).reshape(16, 64, wide)
        fields[tile % 2][pl.ds(step * 16, 16), :, 0:wide] = out

    def pairs(tile, step):
        at, wide = tiles[tile]
        field, out = fields[tile % 2], slopes[tile % 2]
        row = pl.multiple_of(step * 64, 16)
        for lane in range(0, wide, 128):
            scale = wt_ref[0:1, at + lane : at + lane + 128]
            for half in range(0, 64, 8):
                start = pl.multiple_of(row + half, 8)
                true = truth_ref[pl.ds(start, 8), at + lane : at + lane + 128]
                fair_slopes(field, start, lane, true, scale, sums.at[:, at : at + 256])
            for m in range(count):
                out[pl.ds(pl.multiple_of(64 * m + row, 16), 64), lane : lane + 128] = field[
                    m, pl.ds(row, 64), lane : lane + 128
                ].astype(BF16)

    def weight_grad(tile, step):
        at, wide = tiles[tile]
        row = pl.multiple_of(step * 1536, 384)
        out = jnp.dot(
            flipped[pl.ds(row, 1536), :], slopes[tile % 2][:, 0:wide],
            preferred_element_type=F32,
        )
        part[:, 0:wide] = out
        here = out * full_ref[pl.ds(row, 1536), at : at + wide].astype(F32)
        for lane in range(0, wide, 128):
            stop = min(lane + 128, wide)
            rows[pl.ds(row, 1536), 0 : stop - lane] += here[:, lane:stop]
        for q in range(8):
            mine = part[pl.ds(pl.multiple_of(192 * q + core * 96, 96), 96), 0:wide]
            other = part[pl.ds(pl.multiple_of(192 * q + (core ^ 1) * 96, 96), 96), 0:wide]
            keep_ref[8 * step + q, :, at : at + wide] = mine
            start = pl.multiple_of(16 + 96 * (8 * step + q), 16)
            send_ref[pl.ds(start, 96), at : at + wide] = other.astype(BF16)

    for phase in range(len(tiles) + 2):

        def body(step, carry, phase=phase):
            if phase - 2 >= 0:
                weight_grad(phase - 2, step)
            if phase < len(tiles):
                project(phase, step)
            if 0 <= phase - 1 < len(tiles):
                pairs(phase - 1, step)
            return carry

        lax.fori_loop(0, 1, body, 0)
        if 0 <= phase - 1 < len(tiles):
            at, wide = tiles[phase - 1]
            for k in range(8):
                dfield_refs[k][:, at : at + wide] = slopes[(phase - 1) % 2][
                    128 * k : 128 * k + 128, 0:wide
                ]
    small_ref[...] = jnp.zeros_like(small_ref)
    bias_sums = jnp.sum(sums[...], axis=0, keepdims=True)
    for n in range(3):
        turned_rows = jnp.concatenate(
            [rows[512 * n + 128 * q : 512 * n + 128 * q + 128, :].T for q in range(4)], axis=1
        )
        gain_sums = jnp.sum(turned_rows, axis=0, keepdims=True)
        small_ref[n : n + 1, :] = gain_sums / gain_ref[:, 512 * n : 512 * n + 512]
        stop = min(512 * (n + 1), width)
        small_ref[3 + n : 4 + n, 0 : stop - 512 * n] = bias_sums[:, 512 * n : stop]
    put_small(send_ref, small_ref[...])


def backward_kernel(order, before, place_ref, tokens_ref, gain_ref, full_ref, *refs):
    count = len(order)
    earlier, pieces = refs[: len(before)], refs[len(before) : len(before) + count]
    out_ref, dfield, grad = refs[len(before) + count :]
    features = full_ref.shape[0]
    for n in range(count):
        dfield[pl.ds(128 * n, 128), :] = pieces[n][...]

    def matmul(step, carry):
        lane = pl.multiple_of(step * 256, 256)
        grad[:, pl.ds(lane, 256)] = lax.dot_general(
            dfield[...], full_ref[pl.ds(lane, 256), :], (((1,), (1,)), ((), ())),
            preferred_element_type=F32,
        )
        return carry

    lax.fori_loop(0, features // 256, matmul, 0)
    for n, k in enumerate(order):
        j = place_ref[3] ^ k

        def rows(m, carry, n=n, j=j):
            wide = tokens_ref[m, j].astype(F32)
            mean = jnp.mean(wide, -1, keepdims=True)
            centred = wide - mean
            variance = jnp.mean(centred * centred, -1, keepdims=True)
            inverse = lax.rsqrt(variance + EPS)
            xhat = centred * inverse
            start = pl.multiple_of(128 * n + m * 64, 64)
            scaled = grad[pl.ds(start, 64), :] * gain_ref[...]
            out = inverse * (
                scaled
                - jnp.mean(scaled, -1, keepdims=True)
                - xhat * jnp.mean(scaled * xhat, -1, keepdims=True)
            )
            if before:
                out_ref[m, j] = out.astype(BF16)
            else:
                out_ref[n, m] = out.astype(BF16)
            return carry

        lax.fori_loop(0, 2, rows, 0)
    for done, ref in zip(before, earlier):
        for n, k in enumerate(done):
            for m in range(2):
                out_ref[m, place_ref[3] ^ k] = ref[n, m]


def member_rows(parts, where):
    _, _, rows, width = parts.shape
    members = 8 * rows
    index = jnp.arange(members)
    block, inside = index // rows, index % rows
    source = (((block // 2) ^ where["x"]) * 2 + ((block % 2) ^ where["yl"])) * rows + inside
    pick = (source[:, None] == jnp.arange(members)[None, :]).astype(BF16)
    return jnp.dot(
        pick, parts.reshape(members, width), preferred_element_type=F32
    ).astype(BF16)


def put_small(ref, small):
    high = small.astype(BF16)
    low = (small - high.astype(F32)).astype(BF16)
    ref[0:16, :] = jnp.zeros((16, ref.shape[1]), BF16)
    ref[0:16, 0:512] = jnp.concatenate([high, low], axis=0)


def get_small(ref):
    rows = ref[0:16, 0:512].astype(F32)
    return rows[0:8] + rows[8:16]


def core_kernel(place_ref, keep_ref, small_ref, came_ref, own_ref, small_out_ref, *sends):
    small = small_ref[...] + get_small(came_ref)
    small_out_ref[...] = small
    for step in range(4):
        for yh in range(2):
            n = (place_ref[0] ^ yh) * 4 + (place_ref[1] ^ step)
            start = pl.multiple_of(16 + 96 * n, 16)
            block = keep_ref[n] + came_ref[pl.ds(start, 96), :].astype(F32)
            if step == 0:
                own_ref[96 * yh : 96 * yh + 96, :] = block
            else:
                sends[step - 1][16 + 96 * yh : 112 + 96 * yh, :] = block.astype(BF16)
    for ref in sends:
        put_small(ref, small)


def iota(shape, axis):
    return lax.broadcasted_iota(jnp.int32, shape, axis)


def gather_sums(own_ref, small_ref, came):
    total, small = own_ref[...], small_ref[...]
    for ref in came:
        total = total + ref[16 : 16 + own_ref.shape[0], :].astype(F32)
        small = small + get_small(ref)
    return total, small


def z_kernel(own_ref, small_ref, a_ref, b_ref, c_ref, own_out_ref, small_out_ref, send_ref):
    total, small = gather_sums(own_ref, small_ref, (a_ref, b_ref, c_ref))
    small_out_ref[...] = small
    own_out_ref[...] = total[0:96]
    send_ref[16:112, :] = total[96:192].astype(BF16)
    put_small(send_ref, small)


def yh_kernel(own_ref, small_ref, came_ref, out_ref):
    total, small = gather_sums(own_ref, small_ref, (came_ref,))
    row, source = iota((128, 96), 0), iota((128, 96), 1)
    pick = (source == row // 16 * 12 + row % 16) & (row % 16 < 12)
    picked = jnp.dot(
        pick.astype(BF16), total.astype(BF16), preferred_element_type=F32
    ).astype(BF16)
    for n in range(8):
        put_small(out_ref.at[n], small)
        out_ref[n, 16:32, :] = picked[16 * n : 16 * n + 16]


def member_kernel(came_ref, share_ref, gain_out_ref, bias_out_ref):
    total = came_ref[0, 16:32, :].astype(F32)
    small = get_small(came_ref.at[0])
    for n in range(1, 8):
        total = total + came_ref[n, 16:32, :].astype(F32)
        small = small + get_small(came_ref.at[n])
    share_ref[...] = total[0:12]
    for n in range(21):
        ref, at = (gain_out_ref, n) if n < 12 else (bias_out_ref, n - 12)
        ref[at : at + 1, :] = small[n // 4 : n // 4 + 1, 128 * (n % 4) : 128 * (n % 4 + 1)]


def middle(*operands):
    features, outs = 1536, operands[3].shape[1]
    padded = operands[4].shape[1]
    return pl.pallas_call(
        middle_kernel,
        out_shape=(
            jax.ShapeDtypeStruct((features, outs), BF16),
            jax.ShapeDtypeStruct((8, 96, outs), F32),
            jax.ShapeDtypeStruct((16 + 768, outs), BF16),
            jax.ShapeDtypeStruct((8, 512), F32),
        )
        + (jax.ShapeDtypeStruct((128, outs), BF16),) * 8,
        in_specs=[pl.BlockSpec(memory_space=pltpu.SMEM)] + vmem(len(operands) - 1),
        out_specs=tuple(vmem(12)),
        scratch_shapes=[
            pltpu.VMEM((1024, features), BF16),
            pltpu.VMEM((features, 1024), BF16),
            pltpu.VMEM((16, 64, 256), F32),
            pltpu.VMEM((16, 64, 256), F32),
            pltpu.VMEM((1024, 256), BF16),
            pltpu.VMEM((1024, 256), BF16),
            pltpu.VMEM((1536, 256), F32),
            pltpu.VMEM((8, padded + 128), F32),
            pltpu.VMEM((features, 128), F32),
        ],
        compiler_params=params(28),
        cost_estimate=cost(20000000000, 80000000),
        name="middle",
    )(*operands)


def on_device(tokens, gain, weight, bias, target, channel_weight):
    where = {axis: lax.axis_index(axis) for axis in SIZE}
    member = where["x"] * 2 + where["yl"]
    space = (where["yh"] * 4 + where["z"]) * 2 + where["core"]
    place = jnp.stack(
        [where["yh"], where["z"], where["core"], member, where["x"], where["yl"]]
    ).astype(jnp.int32)
    smem = pl.BlockSpec(memory_space=pltpu.SMEM)
    features = tokens.shape[-1]
    outs = weight.shape[1]
    padded = -(-outs // 128) * 128
    gain_row = gain.reshape(1, features)

    pieces = tokens.reshape(2, 8, 64, features)
    sources = [
        lax.dynamic_index_in_dim(pieces, member ^ k, 1, keepdims=False) for k in range(8)
    ]
    t_here, l_here = member // 4, member % 4
    image = lax.dynamic_slice(
        target, (0, 4 * t_here, 256 * l_here), (target.shape[0], 4, 256)
    ).reshape(-1, 256)
    truth = pl.pallas_call(
        truth_kernel,
        out_shape=jax.ShapeDtypeStruct((64, padded), F32),
        in_specs=vmem(1),
        out_specs=vmem(1)[0],
        compiler_params=params(8),
        cost_estimate=cost(2000000000, 8000000),
        name="truth",
    )(image)
    table = jnp.asarray(latitude_weights(128).reshape(32, 4))
    latw = lax.dynamic_index_in_dim(table, space * 2 + t_here, 0, keepdims=False)
    wt = jnp.broadcast_to(
        channel_weight[:, None, None] * latw[None, :, None], (channel_weight.shape[0], 4, 4)
    ).reshape(1, outs)
    wt = jnp.pad(wt, ((0, 0), (0, padded - outs)))

    arrived = {0: sources[0], 4: swap_member(sources[4], 4)}
    near = jnp.stack([weight] + [swap_y(weight, k) for k in (1, 2, 3)])
    (p1,), (near,) = after((sources[1],), near)
    arrived[1] = swap_member(p1, 1)
    wide = jnp.stack([near] + [swap(near, "x", k) for k in (1, 2, 3)])
    (wide, p3, p6), (arrived[4], truth, wt) = after(
        (wide, sources[3], sources[6]), arrived[4], truth, wt
    )
    pair = jnp.stack([member_rows(wide[:, 2 * k : 2 * k + 2], where) for k in range(2)])
    quad = jnp.stack([pair] + [swap(pair, "z", k) for k in (1, 2, 3)])
    arrived[3], arrived[6] = swap_member(p3, 3), swap_member(p6, 6)
    (p7, p2), (arrived[1], arrived[6]) = after(
        (sources[7], sources[2]), arrived[1], arrived[6]
    )
    arrived[7], arrived[2] = swap_member(p7, 7), swap_member(p2, 2)
    (p5,), (arrived[3],) = after((sources[5],), arrived[3])
    arrived[5] = swap_member(p5, 5)
    early = (0, 4, 1, 3, 6)
    normed = {k: norm_piece(arrived[k], gain_row) for k in early}
    held = [n for k in early for n in normed[k]]
    (quad,), done = after((quad,), arrived[7], arrived[2], *held)
    arrived[7], arrived[2] = done[:2]
    for n, k in enumerate(early):
        normed[k] = done[2 + 2 * n : 4 + 2 * n]
    other = swap(quad, "core", 1)
    for k in (7, 2, 5):
        normed[k] = norm_piece(arrived[k], gain_row)

    full, keep, send, small, *dfield = middle(
        place, quad, other, bias.reshape(1, outs), truth, wt, gain_row,
        *[normed[k][0] for k in range(8)], *[normed[k][1] for k in range(8)],
    )

    returned = {0: dfield[0]}
    for k in (1, 4):
        returned[k] = swap_member(dfield[k], k)

    def backward(order, *before):
        count = len(order)
        shape = (2, 8, 64, features) if before else (count, 2, 64, features)
        return pl.pallas_call(
            functools.partial(backward_kernel, order, [done for done, _ in before]),
            out_shape=jax.ShapeDtypeStruct(shape, BF16),
            in_specs=[smem] + vmem(3 + count + len(before)),
            out_specs=vmem(1)[0],
            scratch_shapes=[
                pltpu.VMEM((128 * count, outs), BF16),
                pltpu.VMEM((128 * count, features), F32),
            ],
            compiler_params=params(32),
            cost_estimate=cost(1000, 1000),
            name="backward",
        )(
            place, pieces, gain_row, full,
            *[part for _, part in before], *[returned[k] for k in order],
        )

    def combine(kernel, name, own_rows, send_rows, sends, *operands):
        return pl.pallas_call(
            kernel,
            out_shape=(
                jax.ShapeDtypeStruct((own_rows, outs), F32),
                jax.ShapeDtypeStruct((8, 512), F32),
            )
            + (jax.ShapeDtypeStruct((send_rows, outs), BF16),) * sends,
            in_specs=([smem] if operands[0] is place else [])
            + vmem(len(operands) - (operands[0] is place)),
            out_specs=tuple(vmem(2 + sends)),
            compiler_params=params(16),
            cost_estimate=cost(1000000000, 4000000),
            name=name,
        )(*operands)

    came = swap(send, "core", 1)
    own, small, *sends = combine(core_kernel, "core_sums", 192, 208, 3, place, keep, small, came)
    came = [swap(value, "z", k) for k, value in zip((1, 2, 3), sends)]
    (d3, d6), (small,) = after((dfield[3], dfield[6]), small)
    returned[3], returned[6] = swap_member(d3, 3), swap_member(d6, 6)
    late = (7, 2, 5)
    held, (returned[3], returned[6]) = after(
        [dfield[k] for k in late], returned[3], returned[6]
    )
    for k, piece in zip(late, held):
        returned[k] = swap_member(piece, k)
    first, second = backward(FIRST), backward(SECOND)
    came, (first, second) = after(came, first, second)
    own, small, send = combine(z_kernel, "z_sums", 96, 112, 1, own, small, *came)
    came = swap(send, "yh", 1)
    result = backward(THIRD, (FIRST, first), (SECOND, second))
    (came,), (result,) = after((came,), result)
    send = pl.pallas_call(
        yh_kernel,
        out_shape=jax.ShapeDtypeStruct((8, 32, outs), BF16),
        in_specs=vmem(3),
        out_specs=vmem(1)[0],
        compiler_params=params(16),
        cost_estimate=cost(1000000000, 4000000),
        name="yh_sums",
    )(own, small, came)
    came = lax.all_to_all(send, MEMBER, 0, 0)
    share, gain_sums, bias_sums = pl.pallas_call(
        member_kernel,
        out_shape=(
            jax.ShapeDtypeStruct((12, outs), F32),
            jax.ShapeDtypeStruct((12, 128), F32),
            jax.ShapeDtypeStruct((9, 128), F32),
        ),
        in_specs=vmem(1),
        out_specs=tuple(vmem(3)),
        compiler_params=params(16),
        cost_estimate=cost(1000000000, 4000000),
        name="member_sums",
    )(came)
    return (
        result.reshape(tokens.shape),
        gain_sums.reshape(-1),
        share,
        bias_sums.reshape(-1)[:outs],
    )


def solution(mesh):
    fine = Mesh(
        mesh.devices.reshape(2, 4, 2, 4, 2), ("yh", "z", "core", "x", "yl")
    )
    both = SPACE + MEMBER
    return jax.shard_map(
        on_device,
        mesh=fine,
        in_specs=(
            P(MEMBER, SPACE, None, None),
            P(),
            P(both, None),
            P(),
            P(None, SPACE, None),
            P(),
        ),
        out_specs=(P(MEMBER, SPACE, None, None), P(), P(both, None), P()),
        check_vma=False,
    )
```
